128 devices in a mesh: dp: 2 (over y_lo), head: 8 (over y_hi, x), space: 8 (over z, core).
Axes of the slice: x: 4, y: 4 (y_hi: 2, y_lo: 2; y = y_hi * 2 + y_lo), z: 4, core: 2. Of those that a mesh axis runs over, the one named last changes fastest.
Arguments:
- features: bfloat16 [2, 64, 64, 1280], P('dp', 'space'), may hold values from -96 to 96
- row_map: int32 [64], replicated, may hold values from 0 to 63, as said below
- head_weights: int32 [2, 8], P('dp', 'head'), may hold values from 1 to 3
- ln_gain: float32 [1280], replicated, may hold values from 0.1 to 1.9
- ln_bias: float32 [1280], replicated, may hold values from -3 to 3
- head_in: bfloat16 [8, 1280, 1024], P('head'), may hold values from -0.15625 to 0.15625
- head_bias: float32 [8, 1024], P('head'), may hold values from -4 to 4
- head_out: float32 [8, 1024], P('head'), may hold values from -0.1875 to 0.1875
- patch_embed: bfloat16 [768, 1280], replicated, may hold values from -0.21875 to 0.21875
- act_in: bfloat16 [2, 1024, 1024, 128], P('dp', 'space', 'head'), may hold values from -6 to 6
- act_mid: bfloat16 [2, 1024, 1024, 128], P('dp', 'space', 'head'), may hold values from -6 to 6
- res_conv: bfloat16 [3, 3, 128, 128], replicated, may hold values from -0.1875 to 0.1875
- out_conv: bfloat16 [3, 3, 128, 3], replicated, may hold values from -1.25 to 1.25
Outputs:
- input_grad: bfloat16 [2, 1024, 1024, 128], P('dp', 'space', 'head')
The draws below stay inside these ranges and needn't reach their ends.
Inputs may be any that keep to these rules, and one draw needn't show every extreme that they name: `row_map`: a permutation of the patch rows; each 8 consecutive entries hold equally many rows of every block of 8 consecutive patch rows.
All inputs are finite; a program needn't handle non-finite values.
Results may differ from the reference program's by a relative error of at most 0.017.
Values may be sent and summed in bfloat16 or wider, within the bound.
A program may use at most 192 MiB of HBM per device.

```python
import jax
import jax.numpy as jnp
from jax import lax

IMAGES = 2
HEADS = 8
C = 1280
HID = 1024
CH = 128
PATCH = 16
P3 = 768
PIX_ROWS = 1024
PIX_COLS = 1024
PROWS_DEV = 8
PROWS = 64
PCOLS = 64


def draw_features(key, part):
    key = jax.random.fold_in(key, 11)
    first_key, second_key = jax.random.split(key, 2)
    image_pos = jnp.arange(IMAGES, dtype=jnp.float32) / max(IMAGES - 1, 1)
    row_pos = jnp.arange(PROWS, dtype=jnp.float32) / max(PROWS - 1, 1)
    col_pos = jnp.arange(PCOLS, dtype=jnp.float32) / max(PCOLS - 1, 1)
    trend = 0.5 * jnp.log(3.0) * (image_pos[:, None, None] + row_pos[None, :, None] + col_pos[None, None, :])
    rough = jax.random.uniform(second_key, (IMAGES, PROWS, PCOLS), jnp.float32, 0.0, jnp.log(3.0))
    base = jnp.clip(jax.random.normal(first_key, (IMAGES, PROWS, PCOLS, C), jnp.float32), -6.0, 6.0)
    return (base * jnp.exp(trend + rough)[..., None]).astype(jnp.bfloat16)


def draw_row_map(key, part):
    key = jax.random.fold_in(key, 23)
    first_key, second_key = jax.random.split(key, 2)
    slab_count = PROWS // PROWS_DEV
    per_slab = PROWS_DEV // slab_count
    counter = jnp.arange(PROWS_DEV, dtype=jnp.int32)
    scores = jax.random.randint(first_key, (slab_count, PROWS_DEV), 0, 1048576) * PROWS_DEV + counter
    within = jnp.argsort(scores, axis=1).astype(jnp.int32)
    rows_of = within + (jnp.arange(slab_count, dtype=jnp.int32) * PROWS_DEV)[:, None]
    blocks = rows_of.reshape(slab_count, slab_count, per_slab).transpose(1, 0, 2).reshape(slab_count, PROWS_DEV)
    shuffle = jax.random.randint(second_key, (slab_count, PROWS_DEV), 0, 1048576) * PROWS_DEV + counter
    order = jnp.argsort(shuffle, axis=1).astype(jnp.int32)
    return jnp.take_along_axis(blocks, order, axis=1).reshape(PROWS).astype(jnp.int32)


def touch_ends(entries, rng, least, high):
    longest = entries.shape.index(max(entries.shape))
    spots = []
    for shift in (0, 1):
        where = [jax.random.randint(jax.random.fold_in(rng, axis), (), 0, length) for axis, length in enumerate(entries.shape)]
        where[longest] = (where[longest] + shift) % entries.shape[longest]
        spots.append(tuple(where))
    return entries.at[spots[0]].set(least).at[spots[1]].set(high)


def block_levels(rng, dims, cuts, smallest, high):
    gain = 1.0
    for position, blocks in cuts:
        draws = jax.random.uniform(jax.random.fold_in(jax.random.fold_in(rng, 6), position), (blocks,), jnp.float32, smallest / len(cuts), high / len(cuts))
        gain = gain * jnp.repeat(jnp.exp(draws), dims[position] // blocks).reshape((-1,) + (1,) * (len(dims) - 1 - position))
    return gain


def scatter_about(key, dims, scale, most, cuts=(), held_as=jnp.bfloat16):
    result = jax.random.normal(key, dims, jnp.float32) * scale
    if len(cuts) > 0:
        result = block_levels(key, dims, cuts, -0.22, 0.18) * result
    return jnp.clip(result, min=-most, max=most).astype(held_as)


def setup_inputs(seed: int = 0) -> dict:
    arg_keys = jax.random.split(jax.random.key(seed), 14)
    features = draw_features(jax.random.fold_in(arg_keys[13], 71), 0)
    row_map = draw_row_map(jax.random.fold_in(arg_keys[13], 71), 0)
    head_weights = touch_ends(jax.random.randint(arg_keys[2], (IMAGES, HEADS), 1, 4), jax.random.fold_in(arg_keys[2], 1), 1, 3).astype(jnp.int32)
    ln_gain = jnp.clip(1.0 + 0.18 * jax.random.normal(arg_keys[3], (C,), jnp.float32), 0.1, 1.9)
    ln_bias = scatter_about(arg_keys[4], (C,), 0.5, 3.0, (), jnp.float32)
    head_in = scatter_about(arg_keys[5], (HEADS, C, HID), C ** -0.5, 0.15625, ((0, 8),))
    head_bias = scatter_about(arg_keys[6], (HEADS, HID), 1.0, 4.0, ((0, 8),), jnp.float32)
    head_out = scatter_about(arg_keys[7], (HEADS, HID), HID ** -0.5, 0.1875, ((0, 8),), jnp.float32)
    patch_embed = scatter_about(arg_keys[8], (P3, C), P3 ** -0.5, 0.21875)
    act_in = scatter_about(arg_keys[9], (IMAGES, PIX_ROWS, PIX_COLS, CH), 1.0, 6.0, ((0, 2), (1, 8), (2, 8)))
    act_mid = scatter_about(arg_keys[10], (IMAGES, PIX_ROWS, PIX_COLS, CH), 1.0, 6.0, ((0, 2), (1, 8), (2, 8)))
    res_conv = scatter_about(arg_keys[11], (3, 3, CH, CH), (9 * CH) ** -0.5, 0.1875)
    out_conv = scatter_about(arg_keys[12], (3, 3, CH, 3), 27 ** -0.5, 1.25)
    return dict(features=features, row_map=row_map, head_weights=head_weights, ln_gain=ln_gain, ln_bias=ln_bias, head_in=head_in, head_bias=head_bias, head_out=head_out, patch_embed=patch_embed, act_in=act_in, act_mid=act_mid, res_conv=res_conv, out_conv=out_conv)


def normalize_rows(features, ln_gain, ln_bias):
    values = features.astype(jnp.float32)
    centred = values - lax.optimization_barrier(jnp.mean(values, -1, keepdims=True))
    inverse = lax.rsqrt(lax.optimization_barrier(jnp.mean(centred * centred, -1, keepdims=True)) + 1e-06)
    unit_rows = centred * inverse
    return (unit_rows, inverse, (unit_rows * ln_gain + ln_bias).astype(jnp.bfloat16))

def gelu_slope(values):
    return 0.5 * (1.0 + lax.erf(values * 0.7071067811865476)) + values * jnp.exp(-0.5 * values * values) * 0.3989422804014327

def silu_slope(values):
    sigmoid = jax.nn.sigmoid(values)
    return sigmoid * (1.0 + values * (1.0 - sigmoid))

def norm_backward(gradient, unit_rows, inverse, ln_gain):
    scaled = gradient * ln_gain
    return inverse * (scaled - lax.optimization_barrier(jnp.mean(scaled, -1, keepdims=True)) - unit_rows * lax.optimization_barrier(jnp.mean(scaled * unit_rows, -1, keepdims=True)))

def head_grad(normed, row_weight, first_layer, first_bias, second_layer):
    hidden = jnp.dot(normed, first_layer, preferred_element_type=jnp.float32) + first_bias
    slopes = (row_weight * second_layer * gelu_slope(hidden)).astype(jnp.bfloat16)
    return lax.dot_general(slopes, first_layer, (((1,), (1,)), ((), ())), preferred_element_type=jnp.float32)

def to_pixels(gradient, patch_embed):
    return lax.dot_general(gradient, patch_embed.astype(jnp.float32), (((gradient.ndim - 1,), (1,)), ((), ())), precision=lax.Precision.HIGHEST)

def out_backward(padded, out_conv):
    height = padded.shape[2] - 2
    breadth = padded.shape[3] - 2
    accumulated = jnp.zeros((padded.shape[0], height, breadth, out_conv.shape[2]), jnp.float32)
    for offset_row in range(3):
        for offset_col in range(3):
            window = padded[:, :, offset_row:offset_row + height, offset_col:offset_col + breadth].astype(jnp.float32)
            kernel = out_conv[2 - offset_row, 2 - offset_col].T.astype(jnp.float32)
            accumulated = accumulated + jnp.einsum('norc,ok->nrck', window, kernel)
    return accumulated

def res_backward(padded, res_conv):
    height = padded.shape[1] - 2
    breadth = padded.shape[2] - 2
    channels = res_conv.shape[2]
    accumulated = jnp.zeros((padded.shape[0] * height * breadth, channels), jnp.float32)
    for offset_row in range(3):
        for offset_col in range(3):
            window = padded[:, offset_row:offset_row + height, offset_col:offset_col + breadth].reshape(-1, res_conv.shape[3])
            accumulated = accumulated + jnp.dot(window, res_conv[2 - offset_row, 2 - offset_col].T, preferred_element_type=jnp.float32)
    return accumulated.reshape(padded.shape[0], height, breadth, channels)

def decoder_backward(image_grad, act_in, act_mid, res_conv, out_conv):
    padded = jnp.pad(image_grad, ((0, 0), (0, 0), (1, 1), (1, 1)))
    act_grad = out_backward(padded, out_conv)
    mid_grad = (act_grad * silu_slope(act_mid.astype(jnp.float32))).astype(jnp.bfloat16)
    spread = res_backward(jnp.pad(mid_grad, ((0, 0), (1, 1), (1, 1), (0, 0))), res_conv)
    return (mid_grad.astype(jnp.float32) + silu_slope(act_in.astype(jnp.float32)) * spread).astype(jnp.bfloat16)

def reference(features, row_map, head_weights, ln_gain, ln_bias, head_in, head_bias, head_out, patch_embed, act_in, act_mid, res_conv, out_conv):
    unit_rows, inverse, normed = normalize_rows(features, ln_gain, ln_bias)
    flattened = normed.reshape(-1, C)
    per_image = PROWS * PCOLS

    def one_head(carried, pieces):
        weights, first_layer, first_bias, second_layer = pieces
        row_weight = jnp.repeat(weights.astype(jnp.float32), per_image)[:, None]
        return (carried + head_grad(flattened, row_weight, first_layer, first_bias, second_layer), None)
    summed, unused = lax.scan(one_head, jnp.zeros(flattened.shape, jnp.float32), (head_weights.T, head_in, head_bias, head_out))
    patch_grad = norm_backward(summed.reshape(unit_rows.shape), unit_rows, inverse, ln_gain)
    pixel_grad = to_pixels(patch_grad, patch_embed)
    norm_scale = lax.rsqrt(jnp.mean(pixel_grad * pixel_grad) + 1e-06)
    scaled = (pixel_grad * norm_scale).astype(jnp.bfloat16)
    patches = scaled.reshape(IMAGES, PROWS, PCOLS, 3, PATCH, PATCH)
    patches = jnp.take(patches, jnp.argsort(row_map).astype(jnp.int32), axis=1)
    image_grad = patches.transpose(0, 3, 1, 4, 2, 5).reshape(IMAGES, 3, PIX_ROWS, PIX_COLS)

    def one_image(pieces):
        return decoder_backward(pieces[0][None], pieces[1][None], pieces[2][None], res_conv, out_conv)[0]
    return lax.map(one_image, (image_grad, act_in, act_mid))
```

```python
import functools

import jax
import jax.numpy as jnp
import numpy as np
from jax import lax
from jax.experimental import pallas as pl
from jax.experimental.pallas import tpu as pltpu
from jax.sharding import PartitionSpec as P

MESH = pl.DeviceIdType.MESH
PATCH = 16
P3 = 768
HALF = 384
CH = 128
STRIP = 8
PADC = 160
NT = (((1,), (1,)), ((), ()))
SIDES = ((0, 1), (0, -1), (1, 0), (-1, 0), (1, 1), (-1, 1), (1, -1), (-1, -1))


def spread_table():
    table = np.zeros((P3, PATCH * 128), np.float32)
    for o in range(3):
        for a in range(PATCH):
            for b in range(PATCH):
                table[o * 256 + a * 16 + b, b * 128 + 6 + 3 * a + o] = 1
    return table


def tap_table():
    table = np.zeros((PATCH, 256, 32), np.float32)
    for i in range(PATCH):
        for a in range(3):
            for b in range(3):
                for o in range(3):
                    table[i, 64 * b + 3 * (i + a) + o, (a * 3 + b) * 3 + o] = 1
    return table.reshape(PATCH * 256, 32)


def gelu_slope(v):
    bell = jnp.exp(-0.5 * v * v)
    t = 1.0 / (1.0 + 0.2316418882663604 * jnp.abs(v))
    poly = t * (
        0.127414796
        + t * (-0.142248368 + t * (0.7107068705 + t * (-0.7265760135 + t * 0.5307027145)))
    )
    tail = poly * bell
    return jnp.where(v >= 0, 1.0 - tail, tail) + v * bell * 0.3989422804014327


def silu_slope(v):
    t = jnp.tanh(0.5 * v)
    return 0.5 * (1.0 + t) * (1.0 + 0.5 * v * (1.0 - t))


def stack(values):
    return jnp.concatenate([values[:, :HALF], values[:, HALF:]], axis=0)


def unstack(values):
    return jnp.concatenate([values[:8], values[8:]], axis=1)


def trunk_kernel(
    nd,
    nh,
    ns,
    per,
    row_map,
    weight,
    feats,
    gain_ref,
    shift_ref,
    w_hbm,
    hb_ref,
    ho_ref,
    e_hbm,
    act_mid,
    table,
    x_out,
    sdrow_out,
    sdcol_out,
    total_out,
    f_v,
    w_v,
    e_v,
    t_v,
    strip_v,
    strip_f,
    send,
    recv,
    colmsg,
    rowland,
    colland,
    cornerland,
    hmsg,
    hland,
    pm,
    hp,
    sq1,
    sq2,
    load_sem,
    send_sem,
    recv_sem,
    asend_sem,
    arecv_sem,
    hsend_sem,
    hrecv_sem,
    q_sem,
):
    dp, hd, sp = lax.axis_index("dp"), lax.axis_index("head"), lax.axis_index("space")
    rows = ns * PATCH
    group = nh * ns
    me = hd * ns + sp
    barrier = pltpu.get_barrier_semaphore()

    loads = [
        pltpu.make_async_copy(feats.at[0], f_v, load_sem.at[0]),
        pltpu.make_async_copy(w_hbm.at[0], w_v, load_sem.at[1]),
        pltpu.make_async_copy(e_hbm, e_v, load_sem.at[2]),
        pltpu.make_async_copy(act_mid.at[0, :, pl.ds(0, 16)], strip_v.at[0], load_sem.at[3]),
        pltpu.make_async_copy(act_mid.at[0, :, pl.ds(CH - 16, 16)], strip_v.at[1], load_sem.at[4]),
        pltpu.make_async_copy(table, t_v, load_sem.at[5]),
    ]
    for load in loads:
        load.start()

    def greet(i, carry):
        j = lax.rem(me + i, group)
        pl.semaphore_signal(
            barrier, inc=1, device_id=(dp, lax.div(j, ns), lax.rem(j, ns)), device_id_type=MESH
        )
        return carry

    lax.fori_loop(1, group, greet, 0)

    def greet_far(i, carry):
        pl.semaphore_signal(
            barrier,
            inc=1,
            device_id=(lax.rem(dp + 1 + lax.div(i, ns), nd), hd, lax.rem(i, ns)),
            device_id_type=MESH,
        )
        return carry

    lax.fori_loop(0, (nd - 1) * ns, greet_far, 0)

    loads[0].wait()
    gain = gain_ref[...]
    shift = shift_ref[...]
    second = ho_ref[...] * weight[0, 0].astype(jnp.float32)
    first_bias = hb_ref[...]

    def position(k):
        found = jnp.int32(0)
        for p in range(ns):
            found = found + jnp.where(lax.div(row_map[sp * ns + p], ns) == k, p, 0)
        return jnp.minimum(found, ns - 1)

    def send_rows(i):
        k = lax.rem(sp + 1 + i, ns)
        for j in range(nh):
            h = lax.rem(hd + j, nh)
            if i == ns - 1 and j == 0:
                recv[me] = send[i, h]
            else:
                pltpu.make_async_remote_copy(
                    src_ref=send.at[i, h],
                    dst_ref=recv.at[me],
                    send_sem=send_sem,
                    recv_sem=recv_sem,
                    device_id=(dp, h, k),
                    device_id_type=MESH,
                ).start()

    for chunk in range(ns // per):
        picked = [f_v[position(lax.rem(sp + 1 + chunk * per + t, ns))] for t in range(per)]
        values = jnp.concatenate(picked, axis=0).astype(jnp.float32)
        centred = values - jnp.mean(values, -1, keepdims=True)
        inverse = lax.rsqrt(jnp.mean(centred * centred, -1, keepdims=True) + 1e-06)
        unit = centred * inverse
        normed = (unit * gain + shift).astype(jnp.bfloat16)
        if chunk == 0:
            loads[1].wait()
        hidden = jnp.dot(normed, w_v[...], preferred_element_type=jnp.float32) + first_bias
        slopes = (second * gelu_slope(hidden)).astype(jnp.bfloat16)
        scaled = lax.dot_general(slopes, w_v[...], NT, preferred_element_type=jnp.float32) * gain
        patch = inverse * (
            scaled
            - jnp.mean(scaled, -1, keepdims=True)
            - unit * jnp.mean(scaled * unit, -1, keepdims=True)
        )
        if chunk == 0:
            loads[2].wait()
        pixels = lax.dot_general(
            patch.astype(jnp.bfloat16), e_v[...], NT, preferred_element_type=jnp.float32
        )
        for t in range(per):
            for h in range(nh):
                at = (t * nh + h) * STRIP
                send[chunk * per + t, h] = stack(pixels[at : at + STRIP]).astype(jnp.bfloat16)
        if chunk == 0:
            pl.semaphore_wait(barrier, group - 1 + (nd - 1) * ns)
        for t in range(per):
            send_rows(chunk * per + t)

    loads[3].wait()
    loads[4].wait()
    for side in range(2):
        strip_f[...] = strip_v[side].astype(jnp.float32).reshape(rows * 16, CH)
        colmsg[side] = strip_f[pl.ds(15 * side, rows, stride=16), :].astype(jnp.bfloat16)
    act_copies = []
    for d, (dh, ds) in enumerate(SIDES):
        if dh == 0:
            src, dst = act_mid.at[0, rows - 1 if ds > 0 else 0], rowland.at[d]
        elif ds == 0:
            src, dst = colmsg.at[1 if dh > 0 else 0], colland.at[d - 2]
        else:
            src = act_mid.at[0, rows - 1 if ds > 0 else 0, pl.ds(CH - 16 if dh > 0 else 0, 16)]
            dst = cornerland.at[d - 4]
        act_copies.append(
            pltpu.make_async_remote_copy(
                src_ref=src,
                dst_ref=dst,
                send_sem=asend_sem.at[d],
                recv_sem=arecv_sem.at[d],
                device_id=(dp, lax.rem(hd + dh + nh, nh), lax.rem(sp + ds + ns, ns)),
                device_id_type=MESH,
            )
        )
    for copy in act_copies:
        copy.start()

    def present(dh, ds):
        inside = jnp.bool_(True)
        if dh != 0:
            inside = jnp.logical_and(inside, hd != (0 if dh > 0 else nh - 1))
        if ds != 0:
            inside = jnp.logical_and(inside, sp != (0 if ds > 0 else ns - 1))
        return jnp.where(inside, 1.0, 0.0).astype(jnp.float32)

    for copy in act_copies:
        copy.wait()
    for d, (dh, ds) in enumerate(SIDES):
        there = present(dh, ds)
        if dh == 0:
            sdrow_out[d] = silu_slope(rowland[d].astype(jnp.float32)) * there
        elif ds == 0:
            sdcol_out[d - 2, pl.ds(16, rows), :] = (
                silu_slope(colland[d - 2].astype(jnp.float32)) * there
            )
        else:
            tile = silu_slope(cornerland[d - 4].astype(jnp.float32)) * there
            line = 15 if dh > 0 else 0
            sdcol_out[0 if dh > 0 else 1, pl.ds(15 if ds > 0 else 16 + rows, 1), :] = tile[
                line : line + 1
            ]

    wanted = []
    for s in range(ns):
        r = jnp.int32(0)
        for p in range(ns):
            entry = row_map[s * ns + p]
            r = r + jnp.where(lax.div(entry, ns) == sp, lax.rem(entry, ns), 0)
        wanted.append(r)
    loads[5].wait()
    everything = pltpu.make_async_copy(
        recv.at[pl.ds(0, group - 1)], recv.at[pl.ds(0, group - 1)], recv_sem
    )
    everything.wait()
    squares = jnp.zeros((16, HALF), jnp.float32)
    for r in range(ns):
        source = jnp.int32(0)
        for s in range(ns):
            source = source + jnp.where(wanted[s] == r, s, 0)
        source = jnp.minimum(source, ns - 1)
        summed = recv[source].astype(jnp.float32)
        for h in range(1, nh):
            summed = summed + recv[h * ns + source].astype(jnp.float32)
        squares = squares + summed * summed
        pm[pl.ds(8 * r, 8), :] = unstack(summed)
    squares = squares[:8] + squares[8:]
    sq1[hd] = squares[:, :128] + squares[:, 128:256] + squares[:, 256:]

    lines = jnp.zeros((8, P3), jnp.float32)
    for d, (dh, ds) in enumerate(SIDES):
        r = ns - 1 if ds > 0 else 0
        q = STRIP - 1 if dh > 0 else 0
        if dh == 0:
            message = pm[pl.ds(8 * r, 8), :]
        elif ds == 0:
            parts = [pm[pl.ds(8 * i + q, 1), :] for i in range(ns)]
            if ns < 8:
                parts.append(lines[: 8 - ns])
            message = jnp.concatenate(parts, axis=0)
        else:
            message = jnp.broadcast_to(pm[pl.ds(8 * r + q, 1), :], (8, P3))
        hmsg[d] = stack(message).astype(jnp.bfloat16)
    halo_copies = []
    for d, (dh, ds) in enumerate(SIDES):
        halo_copies.append(
            pltpu.make_async_remote_copy(
                src_ref=hmsg.at[d],
                dst_ref=hland.at[d],
                send_sem=hsend_sem.at[d],
                recv_sem=hrecv_sem.at[d],
                device_id=(dp, lax.rem(hd + dh + nh, nh), lax.rem(sp + ds + ns, ns)),
                device_id_type=MESH,
            )
        )
    for copy in halo_copies:
        copy.start()

    for j in range(1, nh):
        pltpu.make_async_remote_copy(
            src_ref=sq1.at[hd],
            dst_ref=sq1.at[hd],
            send_sem=q_sem.at[0],
            recv_sem=q_sem.at[1],
            device_id=(dp, lax.rem(hd + j, nh), sp),
            device_id_type=MESH,
        ).start()

    spread = jnp.dot(pm[...].astype(jnp.bfloat16), t_v[...], preferred_element_type=jnp.float32)
    for b in range(PATCH):
        for r in range(ns):
            x_out[r + 1, pl.ds(16 + b, 8, stride=16), :] = spread[
                8 * r : 8 * r + 8, 128 * b : 128 * b + 128
            ]

    seven = sq1.at[pl.ds(0, nh - 1)]
    pltpu.make_async_copy(seven, seven, q_sem.at[1]).wait()
    mine = dp * ns + sp
    sq2[mine] = jnp.sum(sq1[...], axis=0)
    for j in range(1, nd * ns):
        other = lax.rem(mine + j, nd * ns)
        pltpu.make_async_remote_copy(
            src_ref=sq2.at[mine],
            dst_ref=sq2.at[mine],
            send_sem=q_sem.at[2],
            recv_sem=q_sem.at[3],
            device_id=(lax.div(other, ns), hd, lax.rem(other, ns)),
            device_id_type=MESH,
        ).start()

    for copy in halo_copies:
        copy.wait()
    for d, (dh, ds) in enumerate(SIDES):
        hp[pl.ds(8 * d, 8), :] = unstack(hland[d].astype(jnp.float32) * present(dh, ds))
    spread = jnp.dot(hp[...].astype(jnp.bfloat16), t_v[...], preferred_element_type=jnp.float32)
    for d, (dh, ds) in enumerate(SIDES):
        r = 0 if ds > 0 else ns + 1
        if dh == 0:
            for b in range(PATCH):
                x_out[r, pl.ds(16 + b, 8, stride=16), :] = spread[
                    8 * d : 8 * d + 8, 128 * b : 128 * b + 128
                ]
            continue
        for b in (PATCH - 2, PATCH - 1) if dh > 0 else (0, 1):
            column = b if dh > 0 else 16 + CH + b
            if ds != 0:
                x_out[r, pl.ds(column, 1), :] = spread[8 * d : 8 * d + 1, 128 * b : 128 * b + 128]
                continue
            for i in range(ns):
                x_out[i + 1, pl.ds(column, 1), :] = spread[
                    8 * d + i : 8 * d + i + 1, 128 * b : 128 * b + 128
                ]

    rest = sq2.at[pl.ds(0, nd * ns - 1)]
    pltpu.make_async_copy(rest, rest, q_sem.at[3]).wait()
    total_out[...] = jnp.sum(sq2[...], axis=0)
    pltpu.make_async_copy(rest, rest, q_sem.at[2]).wait()
    pltpu.make_async_copy(seven, seven, q_sem.at[0]).wait()
    pltpu.make_async_copy(
        recv.at[pl.ds(0, group - 1)], recv.at[pl.ds(0, group - 1)], send_sem
    ).wait()


def decode_kernel(
    ns,
    entries,
    x_ref,
    sdrow,
    sdcol,
    total,
    taps,
    res,
    act_mid,
    act_in,
    out,
    mid_v,
    line_f,
    row_f,
    wr_v,
    am_v,
    ai_v,
    out_v,
    in_sem,
    out_sem,
):
    rows = ns * PATCH
    loads = []
    for i, (src, dst) in enumerate(((act_mid, am_v), (act_in, ai_v))):
        for g in range(ns):
            part = pl.ds(g * PATCH, PATCH)
            loads.append(pltpu.make_async_copy(src.at[0, part], dst.at[part], in_sem.at[i, g]))
    for load in loads:
        load.start()

    for i in range(4):
        for j in range(2):
            for b in range(3):
                a = i - j
                if 0 <= a <= 2:
                    block = res[2 - a, 2 - b]
                else:
                    block = jnp.zeros((CH, CH), jnp.bfloat16)
                wr_v[pl.ds(j * CH, CH), pl.ds((i * 3 + b) * CH, CH)] = block

    lane = lax.broadcasted_iota(jnp.int32, (PADC, 128), 1)

    def pairs(block, count):
        line_f[...] = jnp.where(lane < 6, pltpu.roll(x_ref[block], 80, 1), x_ref[block + 1])
        lhs = jnp.concatenate(
            [
                line_f[pl.ds(7, 144), :] + pltpu.roll(line_f[pl.ds(8, 144), :], 64, 1),
                line_f[pl.ds(9, 144), :],
            ],
            axis=1,
        ).astype(jnp.bfloat16)
        for t in range(count):
            band = jnp.concatenate(
                [taps[pl.ds(512 * t, 256), :], taps[pl.ds(512 * t + 256, 256), :]], axis=1
            )
            act = jnp.dot(lhs, band, preferred_element_type=jnp.float32)
            for i in range(2):
                slot = 2 * t + i
                r = block * PATCH + slot - 1
                grad = act[:, i * CH : (i + 1) * CH]
                if slot == 0:
                    slope = silu_slope(am_v[jnp.maximum(r, 0)].astype(jnp.float32))
                    slope = jnp.where(r < 0, sdrow[0], slope)
                elif count == 1:
                    slope = sdrow[1]
                else:
                    slope = silu_slope(am_v[r].astype(jnp.float32))
                row_f[slot, pl.ds(0, 8), :] = grad[:8] * sdcol[0, pl.ds(r + 16, 1), :]
                row_f[slot, pl.ds(8, CH), :] = grad[8 : 8 + CH] * slope
                row_f[slot, pl.ds(8 + CH, 8), :] = grad[8 + CH :] * sdcol[1, pl.ds(r + 16, 1), :]
                for b in range(3):
                    mid_v[block * 8 + t, :, pl.ds((i * 3 + b) * CH, CH)] = row_f[
                        slot, pl.ds(7 + b, CH), :
                    ].astype(jnp.bfloat16)

    for load in loads[:ns]:
        load.wait()

    def first(block, carry):
        pairs(block, 8)
        return carry

    lax.fori_loop(0, ns, first, 0)
    pairs(ns, 1)

    for load in loads[ns:]:
        load.wait()
    scale = lax.rsqrt(jnp.sum(total[...], keepdims=True) / entries + 1e-06)

    def second(g, carry):
        near = mid_v[pl.ds(8 * g, 8)].reshape(8 * CH, 6 * CH)
        far = mid_v[pl.ds(8 * g + 1, 8)].reshape(8 * CH, 6 * CH)
        spread = lax.dot_general(
            near, wr_v[:, pl.ds(0, 6 * CH)], NT, preferred_element_type=jnp.float32
        ) + lax.dot_general(
            far, wr_v[:, pl.ds(6 * CH, 6 * CH)], NT, preferred_element_type=jnp.float32
        )
        for q in range(8):
            for j in range(2):
                row = g * PATCH + 2 * q + j
                part = spread[q * CH : (q + 1) * CH, j * CH : (j + 1) * CH]
                mid = mid_v[8 * g + q + j, :, pl.ds((4 - 3 * j) * CH, CH)].astype(jnp.float32)
                slope = silu_slope(ai_v[row].astype(jnp.float32))
                out_v[row] = (scale * (mid + slope * part)).astype(jnp.bfloat16)
        part = pl.ds(g * PATCH, PATCH)
        pltpu.make_async_copy(out_v.at[part], out.at[0, part], out_sem).start()
        return carry

    lax.fori_loop(0, ns, second, 0)
    pltpu.make_async_copy(out_v, out.at[0], out_sem).wait()


def local(
    nd,
    nh,
    ns,
    features,
    row_map,
    head_weights,
    ln_gain,
    ln_bias,
    head_in,
    head_bias,
    head_out,
    patch_embed,
    act_in,
    act_mid,
    res_conv,
    out_conv,
):
    C = features.shape[-1]
    HID = head_in.shape[-1]
    rows = ns * PATCH
    group = nh * ns
    per = min(2, ns)
    f32, bf16 = jnp.float32, jnp.bfloat16
    vmem = pl.BlockSpec(memory_space=pltpu.VMEM)
    smem = pl.BlockSpec(memory_space=pltpu.SMEM)
    hbm = pl.BlockSpec(memory_space=pl.ANY)
    x, sdrow, sdcol, total = pl.pallas_call(
        functools.partial(trunk_kernel, nd, nh, ns, per),
        out_shape=(
            jax.ShapeDtypeStruct((ns + 2, PADC, 128), f32),
            jax.ShapeDtypeStruct((2, CH, CH), f32),
            jax.ShapeDtypeStruct((2, rows + 32, CH), f32),
            jax.ShapeDtypeStruct((8, 128), f32),
        ),
        in_specs=[smem, smem, hbm, vmem, vmem, hbm, vmem, vmem, hbm, hbm, hbm],
        out_specs=(vmem,) * 4,
        scratch_shapes=[
            pltpu.VMEM(features.shape[1:], bf16),
            pltpu.VMEM((C, HID), bf16),
            pltpu.VMEM((P3, C), bf16),
            pltpu.VMEM((P3, PATCH * 128), bf16),
            pltpu.VMEM((2, rows, 16, CH), bf16),
            pltpu.VMEM((rows * 16, CH), f32),
            pltpu.VMEM((ns, nh, 16, HALF), bf16),
            pltpu.VMEM((group, 16, HALF), bf16),
            pltpu.VMEM((2, rows, CH), bf16),
            pltpu.VMEM((2, CH, CH), bf16),
            pltpu.VMEM((2, rows, CH), bf16),
            pltpu.VMEM((4, 16, CH), bf16),
            pltpu.VMEM((8, 16, HALF), bf16),
            pltpu.VMEM((8, 16, HALF), bf16),
            pltpu.VMEM((8 * ns, P3), f32),
            pltpu.VMEM((64, P3), f32),
            pltpu.VMEM((nh, 8, 128), f32),
            pltpu.VMEM((nd * ns, 8, 128), f32),
            pltpu.SemaphoreType.DMA((6,)),
            pltpu.SemaphoreType.DMA,
            pltpu.SemaphoreType.DMA,
            pltpu.SemaphoreType.DMA((8,)),
            pltpu.SemaphoreType.DMA((8,)),
            pltpu.SemaphoreType.DMA((8,)),
            pltpu.SemaphoreType.DMA((8,)),
            pltpu.SemaphoreType.DMA((4,)),
        ],
        compiler_params=pltpu.CompilerParams(
            collective_id=0, has_side_effects=True, vmem_limit_bytes=48 * 1024 * 1024
        ),
    )(
        row_map,
        head_weights,
        features,
        ln_gain[None],
        ln_bias[None],
        head_in,
        head_bias,
        head_out,
        patch_embed,
        act_mid,
        jnp.asarray(spread_table(), bf16),
    )

    flat = out_conv[::-1, ::-1].transpose(0, 1, 3, 2).reshape(27, CH)
    taps = jnp.dot(
        jnp.asarray(tap_table(), bf16),
        jnp.pad(flat, ((0, 5), (0, 0))),
        preferred_element_type=f32,
    ).astype(bf16)
    return pl.pallas_call(
        functools.partial(decode_kernel, ns, float(nd * ns * ns * nh * STRIP * P3)),
        out_shape=jax.ShapeDtypeStruct(act_in.shape, bf16),
        in_specs=[vmem] * 6 + [hbm, hbm],
        out_specs=hbm,
        scratch_shapes=[
            pltpu.VMEM((8 * ns + 1, CH, 6 * CH), bf16),
            pltpu.VMEM((PADC, 128), f32),
            pltpu.VMEM((PATCH, 144, 128), f32),
            pltpu.VMEM((2 * CH, 12 * CH), bf16),
            pltpu.VMEM((rows, CH, CH), bf16),
            pltpu.VMEM((rows, CH, CH), bf16),
            pltpu.VMEM((rows, CH, CH), bf16),
            pltpu.SemaphoreType.DMA((2, ns)),
            pltpu.SemaphoreType.DMA,
        ],
        compiler_params=pltpu.CompilerParams(vmem_limit_bytes=56 * 1024 * 1024),
    )(x, sdrow, sdcol, total, taps, res_conv, act_mid, act_in)


def solution(mesh):
    nd, nh, ns = mesh.shape["dp"], mesh.shape["head"], mesh.shape["space"]
    in_specs = (
        P("dp", "space", None, None),
        P(),
        P("dp", "head"),
        P(),
        P(),
        P("head", None, None),
        P("head", None),
        P("head", None),
        P(),
        P("dp", "space", "head", None),
        P("dp", "space", "head", None),
        P(),
        P(),
    )
    out_specs = P("dp", "space", "head", None)
    return jax.shard_map(
        functools.partial(local, nd, nh, ns),
        mesh=mesh,
        in_specs=in_specs,
        out_specs=out_specs,
        check_vma=False,
    )
```

```python
import functools

import jax
import jax.numpy as jnp
from jax import lax
from jax.experimental import pallas as pl
from jax.experimental.pallas import tpu as pltpu
from jax.sharding import PartitionSpec as P

MESH = pl.DeviceIdType.MESH
PATCH = 16
P3 = 768
HALF = 384
CH = 128
STRIP = 8
PADC = 160
NT = (((1,), (1,)), ((), ()))
SIDES = ((0, 1), (0, -1), (1, 0), (-1, 0), (1, 1), (-1, 1), (1, -1), (-1, -1))


def gelu_slope(v):
    bell = jnp.exp(-0.5 * v * v)
    t = 1.0 / (1.0 + 0.2316418882663604 * jnp.abs(v))
    poly = t * (
        0.127414796
        + t * (-0.142248368 + t * (0.7107068705 + t * (-0.7265760135 + t * 0.5307027145)))
    )
    tail = poly * bell
    return jnp.where(v >= 0, 1.0 - tail, tail) + v * bell * 0.3989422804014327


def silu_slope(v):
    half = 0.5 * v.astype(jnp.float32)
    t = jnp.tanh(half)
    return (0.5 + 0.5 * t) * (1.0 + half * (1.0 - t))


def stack(values):
    return jnp.concatenate([values[:, :HALF], values[:, HALF:]], axis=0)


def unstack(values):
    return jnp.concatenate([values[:8], values[8:]], axis=1)


def trunk_kernel(
    nd,
    nh,
    ns,
    order,
    per,
    weight,
    map_hbm,
    feats,
    gain_hbm,
    shift_hbm,
    w_hbm,
    hb_hbm,
    ho_hbm,
    e_hbm,
    act_in,
    act_mid,
    res_hbm,
    tap_hbm,
    mid_out,
    slope_out,
    wr_out,
    total_out,
    row_map,
    f_v,
    w_v,
    e_v,
    t_v,
    g_v,
    b_v,
    hb_v,
    ho_v,
    res_v,
    tap_v,
    band_f,
    band_v,
    am_v,
    normed_v,
    unit_v,
    strip_v,
    strip_f,
    send,
    recv,
    colmsg,
    rowland,
    colland,
    cornerland,
    sdrow,
    sdcol,
    hmsg,
    hland,
    pm,
    hp,
    x_v,
    line_f,
    row_f,
    sq1,
    sq2,
    load_sem,
    act_sem,
    send_sem,
    recv_sem,
    asend_sem,
    arecv_sem,
    hsend_sem,
    hrecv_sem,
    q_sem,
):
    dp, hd, sp = lax.axis_index("dp"), lax.axis_index("head"), lax.axis_index("space")
    rows = ns * PATCH
    group = nh * ns
    me = hd * ns + sp
    barrier = pltpu.get_barrier_semaphore()

    def load(src, dst, i):
        return pltpu.make_async_copy(src, dst, load_sem.at[i])

    load_map = load(map_hbm, row_map, 0)
    load_f = load(feats.at[0], f_v, 1)
    load_g = load(gain_hbm, g_v, 2)
    load_b = load(shift_hbm, b_v, 3)
    load_w = load(w_hbm.at[0], w_v, 4)
    load_hb = load(hb_hbm, hb_v, 5)
    load_ho = load(ho_hbm, ho_v, 6)
    load_e = load(e_hbm, e_v, 7)
    load_near = load(act_mid.at[0, :, pl.ds(0, 16)], strip_v.at[0], 8)
    load_far = load(act_mid.at[0, :, pl.ds(CH - 16, 16)], strip_v.at[1], 9)
    load_res = load(res_hbm, res_v, 10)
    load_tap = load(tap_hbm, tap_v, 11)
    load_mid = pltpu.make_async_copy(act_mid.at[0], am_v, act_sem.at[0])
    load_in = pltpu.make_async_copy(act_in.at[0], slope_out, act_sem.at[1])
    for one in (load_map, load_f, load_g, load_b, load_w, load_hb, load_ho, load_e):
        one.start()

    def greet(i, carry):
        j = lax.rem(me + i, group)
        pl.semaphore_signal(
            barrier, inc=1, device_id=(dp, lax.div(j, ns), lax.rem(j, ns)), device_id_type=MESH
        )
        return carry

    lax.fori_loop(1, group, greet, 0)

    def greet_far(i, carry):
        pl.semaphore_signal(
            barrier,
            inc=1,
            device_id=(lax.rem(dp + 1 + lax.div(i, ns), nd), hd, lax.rem(i, ns)),
            device_id_type=MESH,
        )
        return carry

    lax.fori_loop(0, (nd - 1) * ns, greet_far, 0)

    load_map.wait()
    load_g.wait()
    load_b.wait()
    load_f.wait()
    gain = g_v[...].reshape(1, -1)
    shift = b_v[...].reshape(1, -1)
    cols = nh * STRIP

    def position(k):
        found = jnp.int32(0)
        for p in range(ns):
            found = found + jnp.where(lax.div(row_map[sp * ns + p], ns) == k, p, 0)
        return jnp.minimum(found, ns - 1)

    inverses = []
    for i, step in enumerate(order):
        values = f_v[position(lax.rem(sp + step, ns))].astype(jnp.float32)
        centred = values - jnp.mean(values, -1, keepdims=True)
        inverse = lax.rsqrt(jnp.mean(centred * centred, -1, keepdims=True) + 1e-06)
        unit = centred * inverse
        unit_v[pl.ds(i * cols, cols), :] = unit
        normed_v[pl.ds(i * cols, cols), :] = (unit * gain + shift).astype(jnp.bfloat16)
        inverses.append(inverse)

    load_hb.wait()
    load_ho.wait()
    second = ho_v[...] * weight[0, 0].astype(jnp.float32)
    first_bias = hb_v[...]
    load_w.wait()

    def send_rows(i):
        k = lax.rem(sp + order[i], ns)
        for j in range(nh):
            h = lax.rem(hd + j, nh)
            if order[i] == 0 and j == 0:
                recv[me] = send[i, h]
            else:
                pltpu.make_async_remote_copy(
                    src_ref=send.at[i, h],
                    dst_ref=recv.at[me],
                    send_sem=send_sem,
                    recv_sem=recv_sem,
                    device_id=(dp, h, k),
                    device_id_type=MESH,
                ).start()

    for chunk in range(ns // per):
        part = pl.ds(chunk * per * cols, per * cols)
        hidden = (
            jnp.dot(normed_v[part, :], w_v[...], preferred_element_type=jnp.float32) + first_bias
        )
        slopes = (second * gelu_slope(hidden)).astype(jnp.bfloat16)
        scaled = lax.dot_general(slopes, w_v[...], NT, preferred_element_type=jnp.float32) * gain
        unit = unit_v[part, :]
        inverse = jnp.concatenate(inverses[chunk * per : chunk * per + per], axis=0)
        patch = inverse * (
            scaled
            - jnp.mean(scaled, -1, keepdims=True)
            - unit * jnp.mean(scaled * unit, -1, keepdims=True)
        )
        if chunk == 0:
            load_e.wait()
            for one in (load_near, load_far, load_res, load_tap):
                one.start()
            load_mid.start()
            load_in.start()
        pixels = lax.dot_general(
            patch.astype(jnp.bfloat16), e_v[...], NT, preferred_element_type=jnp.float32
        )
        for t in range(per):
            for h in range(nh):
                at = (t * nh + h) * STRIP
                send[chunk * per + t, h] = stack(pixels[at : at + STRIP]).astype(jnp.bfloat16)
        if chunk == 0:
            pl.semaphore_wait(barrier, group - 1 + (nd - 1) * ns)
        for t in range(per):
            send_rows(chunk * per + t)

    load_near.wait()
    load_far.wait()
    for side in range(2):
        strip_f[...] = strip_v[side].astype(jnp.float32).reshape(rows * 16, CH)
        colmsg[side] = strip_f[pl.ds(15 * side, rows, stride=16), :].astype(jnp.bfloat16)
    act_copies = []
    for d, (dh, ds) in enumerate(SIDES):
        if dh == 0:
            src, dst = act_mid.at[0, rows - 1 if ds > 0 else 0], rowland.at[d]
        elif ds == 0:
            src, dst = colmsg.at[1 if dh > 0 else 0], colland.at[d - 2]
        else:
            src = act_mid.at[0, rows - 1 if ds > 0 else 0, pl.ds(CH - 16 if dh > 0 else 0, 16)]
            dst = cornerland.at[d - 4]
        act_copies.append(
            pltpu.make_async_remote_copy(
                src_ref=src,
                dst_ref=dst,
                send_sem=asend_sem.at[d],
                recv_sem=arecv_sem.at[d],
                device_id=(dp, lax.rem(hd + dh + nh, nh), lax.rem(sp + ds + ns, ns)),
                device_id_type=MESH,
            )
        )
    for copy in act_copies:
        copy.start()

    def present(dh, ds):
        inside = jnp.bool_(True)
        if dh != 0:
            inside = jnp.logical_and(inside, hd != (0 if dh > 0 else nh - 1))
        if ds != 0:
            inside = jnp.logical_and(inside, sp != (0 if ds > 0 else ns - 1))
        return jnp.where(inside, 1.0, 0.0).astype(jnp.float32)

    load_mid.wait()

    def slope_mid(i, carry):
        am_v[pl.ds(4 * i, 4)] = silu_slope(am_v[pl.ds(4 * i, 4)]).astype(jnp.bfloat16)
        return carry

    lax.fori_loop(0, rows // 4, slope_mid, 0)
    load_in.wait()

    def slope_in(i, carry):
        slope_out[pl.ds(4 * i, 4)] = silu_slope(slope_out[pl.ds(4 * i, 4)]).astype(jnp.bfloat16)
        return carry

    lax.fori_loop(0, rows // 4, slope_in, 0)

    line = lax.broadcasted_iota(jnp.int32, (256, 128), 0)
    goal = lax.rem(line, 16) * 64 + 6 + 3 * lax.div(line, 16)
    goal = goal - lax.broadcasted_iota(jnp.int32, (256, 128), 1)
    for o in range(3):
        for i in range(8):
            t_v[pl.ds(256 * o, 256), pl.ds(128 * i, 128)] = jnp.where(
                goal == 128 * i - o, 1.0, 0.0
            ).astype(jnp.bfloat16)

    load_tap.wait()
    load_res.wait()
    band_f[...] = jnp.zeros(band_f.shape, jnp.float32)
    for a in range(3):
        for b in range(3):
            band_f[pl.ds(48 + 64 * b + 3 * a, 3), :] = tap_v[2 - a, 2 - b].astype(jnp.float32)
    for i in range(PATCH):
        band_v[i] = band_f[pl.ds(48 - 3 * i, 256), :].astype(jnp.bfloat16)
    for i in range(4):
        for j in range(2):
            for b in range(3):
                a = i - j
                if 0 <= a <= 2:
                    block = res_v[2 - a, 2 - b]
                else:
                    block = jnp.zeros((CH, CH), jnp.bfloat16)
                wr_out[pl.ds(j * CH, CH), pl.ds((i * 3 + b) * CH, CH)] = block

    for copy in act_copies:
        copy.wait()
    for d, (dh, ds) in enumerate(SIDES):
        there = present(dh, ds)
        if dh == 0:
            sdrow[d] = silu_slope(rowland[d]) * there
        elif ds == 0:
            sdcol[d - 2, pl.ds(16, rows), :] = silu_slope(colland[d - 2]) * there
        else:
            tile = silu_slope(cornerland[d - 4]) * there
            line = 15 if dh > 0 else 0
            sdcol[0 if dh > 0 else 1, pl.ds(15 if ds > 0 else 16 + rows, 1), :] = tile[
                line : line + 1
            ]

    wanted = []
    for s in range(ns):
        r = jnp.int32(0)
        for p in range(ns):
            entry = row_map[s * ns + p]
            r = r + jnp.where(lax.div(entry, ns) == sp, lax.rem(entry, ns), 0)
        wanted.append(r)
    everything = pltpu.make_async_copy(
        recv.at[pl.ds(0, group - 1)], recv.at[pl.ds(0, group - 1)], recv_sem
    )
    everything.wait()
    squares = jnp.zeros((16, HALF), jnp.float32)
    for r in range(ns):
        source = jnp.int32(0)
        for s in range(ns):
            source = source + jnp.where(wanted[s] == r, s, 0)
        source = jnp.minimum(source, ns - 1)
        summed = recv[source].astype(jnp.float32)
        for h in range(1, nh):
            summed = summed + recv[h * ns + source].astype(jnp.float32)
        squares = squares + summed * summed
        pm[pl.ds(8 * r, 8), :] = unstack(summed)

    lines = jnp.zeros((8, P3), jnp.float32)
    for d, (dh, ds) in enumerate(SIDES):
        r = ns - 1 if ds > 0 else 0
        q = STRIP - 1 if dh > 0 else 0
        if dh == 0:
            message = pm[pl.ds(8 * r, 8), :]
        elif ds == 0:
            parts = [pm[pl.ds(8 * i + q, 1), :] for i in range(ns)]
            if ns < 8:
                parts.append(lines[: 8 - ns])
            message = jnp.concatenate(parts, axis=0)
        else:
            message = jnp.broadcast_to(pm[pl.ds(8 * r + q, 1), :], (8, P3))
        hmsg[d] = stack(message).astype(jnp.bfloat16)
    halo_copies = []
    for d, (dh, ds) in enumerate(SIDES):
        halo_copies.append(
            pltpu.make_async_remote_copy(
                src_ref=hmsg.at[d],
                dst_ref=hland.at[d],
                send_sem=hsend_sem.at[d],
                recv_sem=hrecv_sem.at[d],
                device_id=(dp, lax.rem(hd + dh + nh, nh), lax.rem(sp + ds + ns, ns)),
                device_id_type=MESH,
            )
        )
    for copy in halo_copies:
        copy.start()

    squares = squares[:8] + squares[8:]
    sq1[hd] = squares[:, :128] + squares[:, 128:256] + squares[:, 256:]
    for j in range(1, nh):
        pltpu.make_async_remote_copy(
            src_ref=sq1.at[hd],
            dst_ref=sq1.at[hd],
            send_sem=q_sem.at[0],
            recv_sem=q_sem.at[1],
            device_id=(dp, lax.rem(hd + j, nh), sp),
            device_id_type=MESH,
        ).start()

    low = lax.broadcasted_iota(jnp.int32, (8, 128), 1) < 64

    def lanes_of(spread, at, b):
        tile = spread[at : at + 8, 128 * (b // 2) : 128 * (b // 2) + 128]
        if b % 2:
            tile = pltpu.roll(tile, 64, 1)
        return jnp.where(low, tile, 0.0)

    spread = jnp.dot(pm[...].astype(jnp.bfloat16), t_v[...], preferred_element_type=jnp.float32)
    for b in range(PATCH):
        for r in range(ns):
            x_v[r + 1, pl.ds(16 + b, 8, stride=16), :] = lanes_of(spread, 8 * r, b)

    for copy in halo_copies:
        copy.wait()
    for d, (dh, ds) in enumerate(SIDES):
        hp[pl.ds(8 * d, 8), :] = unstack(hland[d].astype(jnp.float32) * present(dh, ds))
    spread = jnp.dot(hp[...].astype(jnp.bfloat16), t_v[...], preferred_element_type=jnp.float32)
    for d, (dh, ds) in enumerate(SIDES):
        r = 0 if ds > 0 else ns + 1
        if dh == 0:
            for b in range(PATCH):
                x_v[r, pl.ds(16 + b, 8, stride=16), :] = lanes_of(spread, 8 * d, b)
            continue
        for b in (PATCH - 2, PATCH - 1) if dh > 0 else (0, 1):
            column = b if dh > 0 else 16 + CH + b
            tile = lanes_of(spread, 8 * d, b)
            if ds != 0:
                x_v[r, pl.ds(column, 1), :] = tile[:1]
                continue
            for i in range(ns):
                x_v[i + 1, pl.ds(column, 1), :] = tile[i : i + 1]

    seven = sq1.at[pl.ds(0, nh - 1)]
    pltpu.make_async_copy(seven, seven, q_sem.at[1]).wait()
    mine = dp * ns + sp
    sq2[mine] = jnp.sum(sq1[...], axis=0)
    for j in range(1, nd * ns):
        other = lax.rem(mine + j, nd * ns)
        pltpu.make_async_remote_copy(
            src_ref=sq2.at[mine],
            dst_ref=sq2.at[mine],
            send_sem=q_sem.at[2],
            recv_sem=q_sem.at[3],
            device_id=(lax.div(other, ns), hd, lax.rem(other, ns)),
            device_id_type=MESH,
        ).start()

    lane = lax.broadcasted_iota(jnp.int32, (PADC, 128), 1)

    def left_side(block, u):
        line_f[u] = jnp.where(lane < 6, pltpu.roll(x_v[block], 80, 1), x_v[block + 1])
        return jnp.concatenate(
            [
                line_f[u, pl.ds(7, 144), :] + pltpu.roll(line_f[u, pl.ds(8, 144), :], 64, 1),
                line_f[u, pl.ds(9, 144), :],
            ],
            axis=1,
        ).astype(jnp.bfloat16)

    def pairs(block, blocks, count):
        lhs = jnp.concatenate([left_side(block + u, u) for u in range(blocks)], axis=0)
        for t in range(count):
            band = jnp.concatenate([band_v[2 * t], band_v[2 * t + 1]], axis=1)
            act = jnp.dot(lhs, band, preferred_element_type=jnp.float32)
            for u in range(blocks):
                for i in range(2):
                    slot = 2 * t + i
                    r = (block + u) * PATCH + slot - 1
                    grad = act[144 * u : 144 * u + 144, i * CH : (i + 1) * CH]
                    if slot == 0 and u == 0 and count > 1:
                        slope = am_v[jnp.maximum(r, 0)].astype(jnp.float32)
                        slope = jnp.where(r < 0, sdrow[0], slope)
                    elif slot == 1 and count == 1:
                        slope = sdrow[1]
                    else:
                        slope = am_v[r].astype(jnp.float32)
                    spot = u * PATCH + slot
                    row_f[spot, pl.ds(0, 8), :] = grad[:8] * sdcol[0, pl.ds(r + 16, 1), :]
                    row_f[spot, pl.ds(8, CH), :] = grad[8 : 8 + CH] * slope
                    row_f[spot, pl.ds(8 + CH, 8), :] = (
                        grad[8 + CH :] * sdcol[1, pl.ds(r + 16, 1), :]
                    )
                    for b in range(3):
                        mid_out[(block + u) * 8 + t, :, pl.ds((i * 3 + b) * CH, CH)] = row_f[
                            spot, pl.ds(7 + b, CH), :
                        ].astype(jnp.bfloat16)

    def first(block, carry):
        pairs(2 * block, 2, 8)
        return carry

    lax.fori_loop(0, ns // 2, first, 0)
    pairs(ns, 1, 1)

    rest = sq2.at[pl.ds(0, nd * ns - 1)]
    pltpu.make_async_copy(rest, rest, q_sem.at[3]).wait()
    total_out[...] = jnp.sum(sq2[...], axis=0)
    pltpu.make_async_copy(rest, rest, q_sem.at[2]).wait()
    pltpu.make_async_copy(seven, seven, q_sem.at[0]).wait()
    pltpu.make_async_copy(
        recv.at[pl.ds(0, group - 1)], recv.at[pl.ds(0, group - 1)], send_sem
    ).wait()


def decode_kernel(ns, entries, mid_ref, slope_ref, wr_ref, total, out, out_v, out_sem):
    scale = lax.rsqrt(jnp.sum(total[...], keepdims=True) / entries + 1e-06)

    def second(g, carry):
        near = mid_ref[pl.ds(8 * g, 8)].reshape(8 * CH, 6 * CH)
        far = mid_ref[pl.ds(8 * g + 1, 8)].reshape(8 * CH, 6 * CH)
        spread = lax.dot_general(
            near, wr_ref[:, pl.ds(0, 6 * CH)], NT, preferred_element_type=jnp.float32
        ) + lax.dot_general(
            far, wr_ref[:, pl.ds(6 * CH, 6 * CH)], NT, preferred_element_type=jnp.float32
        )
        for q in range(8):
            for j in range(2):
                row = g * PATCH + 2 * q + j
                part = spread[q * CH : (q + 1) * CH, j * CH : (j + 1) * CH]
                mid = mid_ref[8 * g + q + j, :, pl.ds((4 - 3 * j) * CH, CH)].astype(jnp.float32)
                slope = slope_ref[row].astype(jnp.float32)
                out_v[row] = (scale * (mid + slope * part)).astype(jnp.bfloat16)
        part = pl.ds(g * PATCH, PATCH)
        pltpu.make_async_copy(out_v.at[part], out.at[0, part], out_sem).start()
        return carry

    lax.fori_loop(0, ns, second, 0)
    pltpu.make_async_copy(out_v, out.at[0], out_sem).wait()


def local(
    nd,
    nh,
    ns,
    features,
    row_map,
    head_weights,
    ln_gain,
    ln_bias,
    head_in,
    head_bias,
    head_out,
    patch_embed,
    act_in,
    act_mid,
    res_conv,
    out_conv,
):
    C = features.shape[-1]
    HID = head_in.shape[-1]
    rows = ns * PATCH
    group = nh * ns
    patches = ns * nh * STRIP
    order = [s % ns for s in (2, -2, 3, -3, 4, 1, -1)]
    order = [s for i, s in enumerate(order) if s and s not in order[:i]] + [0]
    per = max(1, ns // 2)
    f32, bf16 = jnp.float32, jnp.bfloat16
    vmem = pl.BlockSpec(memory_space=pltpu.VMEM)
    smem = pl.BlockSpec(memory_space=pltpu.SMEM)
    hbm = pl.BlockSpec(memory_space=pl.ANY)
    dma = pltpu.SemaphoreType.DMA
    mid, slope, wr, total = pl.pallas_call(
        functools.partial(trunk_kernel, nd, nh, ns, order, per),
        out_shape=(
            pltpu.VMEM((8 * ns + 1, CH, 6 * CH), bf16),
            pltpu.VMEM((rows, CH, CH), bf16),
            pltpu.VMEM((2 * CH, 12 * CH), bf16),
            pltpu.VMEM((8, 128), f32),
        ),
        in_specs=[smem] + [pl.BlockSpec(memory_space=pltpu.HBM)] * 12,
        out_specs=(vmem,) * 4,
        scratch_shapes=[
            pltpu.SMEM(row_map.shape, jnp.int32),
            pltpu.VMEM(features.shape[1:], bf16),
            pltpu.VMEM((C, HID), bf16),
            pltpu.VMEM((P3, C), bf16),
            pltpu.VMEM((P3, PATCH * 64), bf16),
            pltpu.VMEM((C,), f32),
            pltpu.VMEM((C,), f32),
            pltpu.VMEM((1, HID), f32),
            pltpu.VMEM((1, HID), f32),
            pltpu.VMEM(res_conv.shape, bf16),
            pltpu.VMEM((3, 3, 3, CH), bf16),
            pltpu.VMEM((304, CH), f32),
            pltpu.VMEM((PATCH, 256, CH), bf16),
            pltpu.VMEM((rows, CH, CH), bf16),
            pltpu.VMEM((patches, C), bf16),
            pltpu.VMEM((patches, C), f32),
            pltpu.VMEM((2, rows, 16, CH), bf16),
            pltpu.VMEM((rows * 16, CH), f32),
            pltpu.VMEM((ns, nh, 16, HALF), bf16),
            pltpu.VMEM((group, 16, HALF), bf16),
            pltpu.VMEM((2, rows, CH), bf16),
            pltpu.VMEM((2, CH, CH), bf16),
            pltpu.VMEM((2, rows, CH), bf16),
            pltpu.VMEM((4, 16, CH), bf16),
            pltpu.VMEM((2, CH, CH), f32),
            pltpu.VMEM((2, rows + 32, CH), f32),
            pltpu.VMEM((8, 16, HALF), bf16),
            pltpu.VMEM((8, 16, HALF), bf16),
            pltpu.VMEM((8 * ns, P3), f32),
            pltpu.VMEM((64, P3), f32),
            pltpu.VMEM((ns + 2, PADC, 128), f32),
            pltpu.VMEM((2, PADC, 128), f32),
            pltpu.VMEM((2 * PATCH, 144, 128), f32),
            pltpu.VMEM((nh, 8, 128), f32),
            pltpu.VMEM((nd * ns, 8, 128), f32),
            dma((12,)),
            dma((2,)),
            dma,
            dma,
            dma((8,)),
            dma((8,)),
            dma((8,)),
            dma((8,)),
            dma((4,)),
        ],
        compiler_params=pltpu.CompilerParams(
            collective_id=0, has_side_effects=True, vmem_limit_bytes=40 * 1024 * 1024
        ),
    )(
        head_weights,
        row_map,
        features,
        ln_gain,
        ln_bias,
        head_in,
        head_bias,
        head_out,
        patch_embed,
        act_in,
        act_mid,
        res_conv,
        out_conv.transpose(0, 1, 3, 2),
    )
    return pl.pallas_call(
        functools.partial(decode_kernel, ns, float(nd * ns * ns * nh * STRIP * P3)),
        out_shape=jax.ShapeDtypeStruct(act_in.shape, bf16),
        in_specs=[vmem] * 4,
        out_specs=hbm,
        scratch_shapes=[pltpu.VMEM((rows, CH, CH), bf16), dma],
        compiler_params=pltpu.CompilerParams(vmem_limit_bytes=16 * 1024 * 1024),
    )(mid, slope, wr, total)


def solution(mesh):
    nd, nh, ns = mesh.shape["dp"], mesh.shape["head"], mesh.shape["space"]
    in_specs = (
        P("dp", "space", None, None),
        P(),
        P("dp", "head"),
        P(),
        P(),
        P("head", None, None),
        P("head", None),
        P("head", None),
        P(),
        P("dp", "space", "head", None),
        P("dp", "space", "head", None),
        P(),
        P(),
    )
    out_specs = P("dp", "space", "head", None)
    return jax.shard_map(
        functools.partial(local, nd, nh, ns),
        mesh=mesh,
        in_specs=in_specs,
        out_specs=out_specs,
        check_vma=False,
    )
```

```python
import functools

import jax
import jax.numpy as jnp
from jax import lax
from jax.experimental import pallas as pl
from jax.experimental.pallas import tpu as pltpu
from jax.sharding import PartitionSpec as P

MESH = pl.DeviceIdType.MESH
PATCH = 16
P3 = 768
HALF = 384
CH = 128
STRIP = 8
PADC = 160
NT = (((1,), (1,)), ((), ()))
SIDES = ((0, 1), (0, -1), (1, 0), (-1, 0), (1, 1), (-1, 1), (1, -1), (-1, -1))


def gelu_slope(v):
    bell = jnp.exp(-0.5 * v * v)
    t = 1.0 / (1.0 + 0.2316418882663604 * jnp.abs(v))
    poly = t * (
        0.127414796
        + t * (-0.142248368 + t * (0.7107068705 + t * (-0.7265760135 + t * 0.5307027145)))
    )
    tail = poly * bell
    return jnp.where(v >= 0, 1.0 - tail, tail) + v * bell * 0.3989422804014327


def silu_slope(v):
    half = 0.5 * v.astype(jnp.float32)
    t = jnp.tanh(half)
    return (0.5 + 0.5 * t) * (1.0 + half * (1.0 - t))


def stack(values):
    return jnp.concatenate([values[:, :HALF], values[:, HALF:]], axis=0)


def unstack(values):
    return jnp.concatenate([values[:8], values[8:]], axis=1)


def trunk_kernel(
    nd,
    nh,
    ns,
    order,
    per,
    weight,
    map_hbm,
    feats,
    gain_hbm,
    shift_hbm,
    w_hbm,
    hb_hbm,
    ho_hbm,
    e_hbm,
    act_in,
    act_mid,
    res_hbm,
    tap_hbm,
    mid_out,
    slope_out,
    wr_out,
    total_out,
    row_map,
    f_v,
    w_v,
    e_v,
    t_v,
    g_v,
    b_v,
    hb_v,
    ho_v,
    res_v,
    tap_v,
    band_f,
    band_v,
    am_v,
    normed_v,
    unit_v,
    strip_f,
    send,
    recv,
    colmsg,
    rowland,
    colland,
    cornerland,
    sdrow,
    sdcol,
    hmsg,
    hland,
    pm,
    hp,
    x_v,
    line_f,
    row_f,
    edge_v,
    fix_f,
    sq1,
    sq2,
    load_sem,
    act_sem,
    send_sem,
    recv_sem,
    asend_sem,
    arecv_sem,
    hsend_sem,
    hrecv_sem,
    q_sem,
):
    dp, hd, sp = lax.axis_index("dp"), lax.axis_index("head"), lax.axis_index("space")
    rows = ns * PATCH
    group = nh * ns
    me = hd * ns + sp
    barrier = pltpu.get_barrier_semaphore()

    def load(src, dst, i):
        return pltpu.make_async_copy(src, dst, load_sem.at[i])

    load_map = load(map_hbm, row_map, 0)
    load_f = load(feats.at[0], f_v, 1)
    load_g = load(gain_hbm, g_v, 2)
    load_b = load(shift_hbm, b_v, 3)
    load_w = load(w_hbm.at[0], w_v, 4)
    load_hb = load(hb_hbm, hb_v, 5)
    load_ho = load(ho_hbm, ho_v, 6)
    load_e = load(e_hbm, e_v, 7)
    load_res = load(res_hbm, res_v, 8)
    load_tap = load(tap_hbm, tap_v, 9)
    load_mid = pltpu.make_async_copy(act_mid.at[0], am_v, act_sem.at[0])
    load_in = pltpu.make_async_copy(act_in.at[0], slope_out, act_sem.at[1])
    for one in (load_map, load_f, load_g, load_b, load_w, load_hb, load_ho, load_e):
        one.start()

    def greet(i, carry):
        j = lax.rem(me + i, group)
        pl.semaphore_signal(
            barrier, inc=1, device_id=(dp, lax.div(j, ns), lax.rem(j, ns)), device_id_type=MESH
        )
        return carry

    lax.fori_loop(1, group, greet, 0)

    def greet_far(i, carry):
        pl.semaphore_signal(
            barrier,
            inc=1,
            device_id=(lax.rem(dp + 1 + lax.div(i, ns), nd), hd, lax.rem(i, ns)),
            device_id_type=MESH,
        )
        return carry

    lax.fori_loop(0, (nd - 1) * ns, greet_far, 0)

    load_map.wait()
    load_g.wait()
    load_b.wait()
    load_f.wait()
    gain = g_v[...].reshape(1, -1)
    shift = b_v[...].reshape(1, -1)
    cols = nh * STRIP

    def position(k):
        found = jnp.int32(0)
        for p in range(ns):
            found = found + jnp.where(lax.div(row_map[sp * ns + p], ns) == k, p, 0)
        return jnp.minimum(found, ns - 1)

    inverses = []
    for i, step in enumerate(order):
        values = f_v[position(lax.rem(sp + step, ns))].astype(jnp.float32)
        centred = values - jnp.mean(values, -1, keepdims=True)
        inverse = lax.rsqrt(jnp.mean(centred * centred, -1, keepdims=True) + 1e-06)
        unit = centred * inverse
        unit_v[pl.ds(i * cols, cols), :] = unit
        normed_v[pl.ds(i * cols, cols), :] = (unit * gain + shift).astype(jnp.bfloat16)
        inverses.append(inverse)

    load_hb.wait()
    load_ho.wait()
    second = ho_v[...] * weight[0, 0].astype(jnp.float32)
    first_bias = hb_v[...]
    load_w.wait()

    def send_rows(i):
        k = lax.rem(sp + order[i], ns)
        for j in range(nh):
            h = lax.rem(hd + j, nh)
            if order[i] == 0 and j == 0:
                recv[me] = send[i, h]
            else:
                pltpu.make_async_remote_copy(
                    src_ref=send.at[i, h],
                    dst_ref=recv.at[me],
                    send_sem=send_sem,
                    recv_sem=recv_sem,
                    device_id=(dp, h, k),
                    device_id_type=MESH,
                ).start()

    for chunk in range(ns // per):
        part = pl.ds(chunk * per * cols, per * cols)
        hidden = (
            jnp.dot(normed_v[part, :], w_v[...], preferred_element_type=jnp.float32) + first_bias
        )
        slopes = (second * gelu_slope(hidden)).astype(jnp.bfloat16)
        scaled = lax.dot_general(slopes, w_v[...], NT, preferred_element_type=jnp.float32) * gain
        unit = unit_v[part, :]
        inverse = jnp.concatenate(inverses[chunk * per : chunk * per + per], axis=0)
        patch = inverse * (
            scaled
            - jnp.mean(scaled, -1, keepdims=True)
            - unit * jnp.mean(scaled * unit, -1, keepdims=True)
        )
        if chunk == 0:
            load_e.wait()
            for one in (load_res, load_tap):
                one.start()
            load_mid.start()
            load_in.start()
        pixels = lax.dot_general(
            patch.astype(jnp.bfloat16), e_v[...], NT, preferred_element_type=jnp.float32
        )
        for t in range(per):
            for h in range(nh):
                at = (t * nh + h) * STRIP
                send[chunk * per + t, h] = stack(pixels[at : at + STRIP]).astype(jnp.bfloat16)
        if chunk == 0:
            pl.semaphore_wait(barrier, group - 1 + (nd - 1) * ns)
        for t in range(per):
            send_rows(chunk * per + t)

    def present(dh, ds):
        inside = jnp.bool_(True)
        if dh != 0:
            inside = jnp.logical_and(inside, hd != (0 if dh > 0 else nh - 1))
        if ds != 0:
            inside = jnp.logical_and(inside, sp != (0 if ds > 0 else ns - 1))
        return jnp.where(inside, 1.0, 0.0).astype(jnp.float32)

    load_mid.wait()

    def slope_mid(i, carry):
        am_v[pl.ds(4 * i, 4)] = silu_slope(am_v[pl.ds(4 * i, 4)]).astype(jnp.bfloat16)
        return carry

    lax.fori_loop(0, rows // 4, slope_mid, 0)
    for side in range(2):
        edge = am_v[:, pl.ds((CH - 16) * side, 16), :].astype(jnp.float32)
        strip_f[...] = edge.reshape(rows * 16, CH)
        colmsg[side] = strip_f[pl.ds(15 * side, rows, stride=16), :].astype(jnp.bfloat16)
    load_in.wait()

    def slope_in(i, carry):
        slope_out[pl.ds(4 * i, 4)] = silu_slope(slope_out[pl.ds(4 * i, 4)]).astype(jnp.bfloat16)
        return carry

    lax.fori_loop(0, rows // 4, slope_in, 0)

    line = lax.broadcasted_iota(jnp.int32, (256, 128), 0)
    goal = lax.rem(line, 16) * 64 + 6 + 3 * lax.div(line, 16)
    goal = goal - lax.broadcasted_iota(jnp.int32, (256, 128), 1)
    for o in range(3):
        for i in range(8):
            t_v[pl.ds(256 * o, 256), pl.ds(128 * i, 128)] = jnp.where(
                goal == 128 * i - o, 1.0, 0.0
            ).astype(jnp.bfloat16)

    load_tap.wait()
    load_res.wait()
    band_f[...] = jnp.zeros(band_f.shape, jnp.float32)
    for a in range(3):
        for b in range(3):
            band_f[pl.ds(48 + 64 * b + 3 * a, 3), :] = tap_v[2 - a, 2 - b].astype(jnp.float32)
    for i in range(PATCH):
        band_v[i] = band_f[pl.ds(48 - 3 * i, 256), :].astype(jnp.bfloat16)
    for i in range(4):
        for j in range(2):
            for b in range(3):
                a = i - j
                if 0 <= a <= 2:
                    block = res_v[2 - a, 2 - b].astype(jnp.float32).T.astype(jnp.bfloat16)
                else:
                    block = jnp.zeros((CH, CH), jnp.bfloat16)
                wr_out[pl.ds((i * 3 + b) * CH, CH), pl.ds(j * CH, CH)] = block

    wanted = []
    for s in range(ns):
        r = jnp.int32(0)
        for p in range(ns):
            entry = row_map[s * ns + p]
            r = r + jnp.where(lax.div(entry, ns) == sp, lax.rem(entry, ns), 0)
        wanted.append(r)
    everything = pltpu.make_async_copy(
        recv.at[pl.ds(0, group - 1)], recv.at[pl.ds(0, group - 1)], recv_sem
    )
    everything.wait()
    squares = jnp.zeros((16, HALF), jnp.float32)
    for r in range(ns):
        source = jnp.int32(0)
        for s in range(ns):
            source = source + jnp.where(wanted[s] == r, s, 0)
        source = jnp.minimum(source, ns - 1)
        summed = recv[source].astype(jnp.float32)
        for h in range(1, nh):
            summed = summed + recv[h * ns + source].astype(jnp.float32)
        squares = squares + summed * summed
        pm[pl.ds(8 * r, 8), :] = unstack(summed)

    lines = jnp.zeros((8, P3), jnp.float32)
    for d, (dh, ds) in enumerate(SIDES):
        r = ns - 1 if ds > 0 else 0
        q = STRIP - 1 if dh > 0 else 0
        if dh == 0:
            message = pm[pl.ds(8 * r, 8), :]
        elif ds == 0:
            parts = [pm[pl.ds(8 * i + q, 1), :] for i in range(ns)]
            if ns < 8:
                parts.append(lines[: 8 - ns])
            message = jnp.concatenate(parts, axis=0)
        else:
            message = jnp.broadcast_to(pm[pl.ds(8 * r + q, 1), :], (8, P3))
        hmsg[d] = stack(message).astype(jnp.bfloat16)
    halo_copies = []
    for d, (dh, ds) in enumerate(SIDES):
        halo_copies.append(
            pltpu.make_async_remote_copy(
                src_ref=hmsg.at[d],
                dst_ref=hland.at[d],
                send_sem=hsend_sem.at[d],
                recv_sem=hrecv_sem.at[d],
                device_id=(dp, lax.rem(hd + dh + nh, nh), lax.rem(sp + ds + ns, ns)),
                device_id_type=MESH,
            )
        )
    for copy in halo_copies:
        copy.start()

    squares = squares[:8] + squares[8:]
    sq1[hd] = squares[:, :128] + squares[:, 128:256] + squares[:, 256:]
    for j in range(1, nh):
        pltpu.make_async_remote_copy(
            src_ref=sq1.at[hd],
            dst_ref=sq1.at[hd],
            send_sem=q_sem.at[0],
            recv_sem=q_sem.at[1],
            device_id=(dp, lax.rem(hd + j, nh), sp),
            device_id_type=MESH,
        ).start()

    act_copies = []
    for d, (dh, ds) in enumerate(SIDES):
        if dh == 0:
            src, dst = am_v.at[rows - 1 if ds > 0 else 0], rowland.at[d]
        elif ds == 0:
            src, dst = colmsg.at[1 if dh > 0 else 0], colland.at[d - 2]
        else:
            src = am_v.at[rows - 1 if ds > 0 else 0, pl.ds(CH - 16 if dh > 0 else 0, 16)]
            dst = cornerland.at[d - 4]
        act_copies.append(
            pltpu.make_async_remote_copy(
                src_ref=src,
                dst_ref=dst,
                send_sem=asend_sem.at[d],
                recv_sem=arecv_sem.at[d],
                device_id=(dp, lax.rem(hd + dh + nh, nh), lax.rem(sp + ds + ns, ns)),
                device_id_type=MESH,
            )
        )
    for copy in act_copies:
        copy.start()

    low = lax.broadcasted_iota(jnp.int32, (8, 128), 1) < 64

    def lanes_of(spread, at, b):
        tile = spread[at : at + 8, 128 * (b // 2) : 128 * (b // 2) + 128]
        if b % 2:
            tile = pltpu.roll(tile, 64, 1)
        return jnp.where(low, tile, 0.0)

    spread = jnp.dot(pm[...].astype(jnp.bfloat16), t_v[...], preferred_element_type=jnp.float32)
    for b in range(PATCH):
        for r in range(ns):
            x_v[r + 1, pl.ds(16 + b, 8, stride=16), :] = lanes_of(spread, 8 * r, b)

    x_v[0] = jnp.zeros((PADC, 128), jnp.float32)
    lane = lax.broadcasted_iota(jnp.int32, (PADC, 128), 1)

    def set_line(block, u):
        line_f[u] = jnp.where(lane < 6, pltpu.roll(x_v[block], 80, 1), x_v[block + 1])

    def left_side(u, start, size):
        return jnp.concatenate(
            [
                line_f[u, pl.ds(start - 1, size), :]
                + pltpu.roll(line_f[u, pl.ds(start, size), :], 64, 1),
                line_f[u, pl.ds(start + 1, size), :],
            ],
            axis=1,
        ).astype(jnp.bfloat16)

    def inner(step, carry):
        block = 2 * step
        for u in range(2):
            set_line(block + u, u)
        lhs = jnp.concatenate([left_side(u, 16, CH) for u in range(2)], axis=0)
        for t in range(8):
            band = jnp.concatenate([band_v[2 * t], band_v[2 * t + 1]], axis=1)
            act = jnp.dot(lhs, band, preferred_element_type=jnp.float32)
            for u in range(2):
                for i in range(2):
                    slot = 2 * t + i
                    r = jnp.maximum((block + u) * PATCH + slot - 1, 0)
                    spot = u * PATCH + slot
                    row_f[spot, pl.ds(8, CH), :] = act[
                        CH * u : CH * u + CH, i * CH : (i + 1) * CH
                    ] * am_v[r].astype(jnp.float32)
                    for b in range(3):
                        mid_out[(block + u) * 8 + t, i * 3 + b] = row_f[
                            spot, pl.ds(7 + b, CH), :
                        ].astype(jnp.bfloat16)
        return carry

    row_f[:, pl.ds(0, 8), :] = jnp.zeros((2 * PATCH, 8, 128), jnp.float32)
    row_f[:, pl.ds(8 + CH, 8), :] = jnp.zeros((2 * PATCH, 8, 128), jnp.float32)
    half = ns // 2
    lax.fori_loop(0, half - half // 4, inner, 0)

    seven = sq1.at[pl.ds(0, nh - 1)]
    pltpu.make_async_copy(seven, seven, q_sem.at[1]).wait()
    mine = dp * ns + sp
    sq2[mine] = jnp.sum(sq1[...], axis=0)
    for j in range(1, nd * ns):
        other = lax.rem(mine + j, nd * ns)
        pltpu.make_async_remote_copy(
            src_ref=sq2.at[mine],
            dst_ref=sq2.at[mine],
            send_sem=q_sem.at[2],
            recv_sem=q_sem.at[3],
            device_id=(lax.div(other, ns), hd, lax.rem(other, ns)),
            device_id_type=MESH,
        ).start()

    lax.fori_loop(half - half // 4, half, inner, 0)

    for copy in halo_copies:
        copy.wait()
    for d, (dh, ds) in enumerate(SIDES):
        hp[pl.ds(8 * d, 8), :] = unstack(hland[d].astype(jnp.float32) * present(dh, ds))
    spread = jnp.dot(hp[...].astype(jnp.bfloat16), t_v[...], preferred_element_type=jnp.float32)
    for d, (dh, ds) in enumerate(SIDES):
        r = 0 if ds > 0 else ns + 1
        if dh == 0:
            for b in range(PATCH):
                x_v[r, pl.ds(16 + b, 8, stride=16), :] = lanes_of(spread, 8 * d, b)
            continue
        for b in (PATCH - 2, PATCH - 1) if dh > 0 else (0, 1):
            column = b if dh > 0 else 16 + CH + b
            tile = lanes_of(spread, 8 * d, b)
            if ds != 0:
                x_v[r, pl.ds(column, 1), :] = tile[:1]
                continue
            for i in range(ns):
                x_v[i + 1, pl.ds(column, 1), :] = tile[i : i + 1]
    for copy in act_copies:
        copy.wait()
    for d, (dh, ds) in enumerate(SIDES):
        there = present(dh, ds)
        if dh == 0:
            sdrow[d] = rowland[d].astype(jnp.float32) * there
        elif ds == 0:
            sdcol[d - 2, pl.ds(16, rows), :] = colland[d - 2].astype(jnp.float32) * there
        else:
            tile = cornerland[d - 4].astype(jnp.float32) * there
            line = 15 if dh > 0 else 0
            sdcol[0 if dh > 0 else 1, pl.ds(15 if ds > 0 else 16 + rows, 1), :] = tile[
                line : line + 1
            ]

    for block in range(ns):
        set_line(block, block)
        for side in range(2):
            edge_v[pl.ds(64 * block + 32 * side, 32), :] = left_side(block, 8 + 112 * side, 32)

    def edges(t, carry):
        band = jnp.concatenate([band_v[2 * t], band_v[2 * t + 1]], axis=1)
        act = jnp.dot(edge_v[...], band, preferred_element_type=jnp.float32)
        for block in range(ns):
            for i in range(2):
                row = block * PATCH + 2 * t + i - 1
                inside = jnp.maximum(row, 0)
                for side in range(2):
                    spot = (block * 2 + i) * 2 + side
                    at = 64 * block + 32 * side
                    grad = act[at : at + 32, i * CH : (i + 1) * CH]
                    slope = am_v[inside, pl.ds((CH - 32) * side, 32), :].astype(jnp.float32)
                    beyond = sdcol[side, pl.ds(row + 16, 1), :]
                    if side == 0:
                        fix_f[spot, pl.ds(0, 8), :] = grad[:8] * beyond
                        fix_f[spot, pl.ds(8, 24), :] = grad[8:] * slope[:24]
                    else:
                        fix_f[spot, pl.ds(0, 24), :] = grad[:24] * slope[8:]
                        fix_f[spot, pl.ds(24, 8), :] = grad[24:] * beyond
                    for b in range(3):
                        mid_out[block * 8 + t, i * 3 + b, pl.ds((CH - 16) * side, 16), :] = fix_f[
                            spot, pl.ds(7 + b, 16), :
                        ].astype(jnp.bfloat16)
        return carry

    lax.fori_loop(0, 8, edges, 0)

    set_line(ns, ns)
    band = jnp.concatenate([band_v[0], band_v[1]], axis=1)
    lhs = jnp.concatenate([left_side(0, 8, 144), left_side(ns, 8, 144)], axis=0)
    act = jnp.dot(lhs, band, preferred_element_type=jnp.float32)
    for u in range(2):
        for i in range(2):
            row = u * rows + i - 1
            grad = act[144 * u : 144 * u + 144, i * CH : (i + 1) * CH]
            if u == i:
                slope = sdrow[u]
            else:
                slope = am_v[row].astype(jnp.float32)
            spot = 2 * u + i
            row_f[spot, pl.ds(0, 8), :] = grad[:8] * sdcol[0, pl.ds(row + 16, 1), :]
            row_f[spot, pl.ds(8, CH), :] = grad[8 : 8 + CH] * slope
            row_f[spot, pl.ds(8 + CH, 8), :] = grad[8 + CH :] * sdcol[1, pl.ds(row + 16, 1), :]
            for b in range(3):
                mid_out[u * ns * 8, i * 3 + b] = row_f[spot, pl.ds(7 + b, CH), :].astype(
                    jnp.bfloat16
                )

    rest = sq2.at[pl.ds(0, nd * ns - 1)]
    pltpu.make_async_copy(rest, rest, q_sem.at[3]).wait()
    total_out[...] = jnp.sum(sq2[...], axis=0)
    pltpu.make_async_copy(rest, rest, q_sem.at[2]).wait()
    pltpu.make_async_copy(seven, seven, q_sem.at[0]).wait()
    pltpu.make_async_copy(
        recv.at[pl.ds(0, group - 1)], recv.at[pl.ds(0, group - 1)], send_sem
    ).wait()


def decode_kernel(ns, entries, mid_ref, slope_ref, wr_ref, total, out, out_v, out_sem):
    scale = lax.rsqrt(jnp.sum(total[...], keepdims=True) / entries + 1e-06)
    size = min(16, 8 * ns)

    def step(g, carry):
        terms = []
        for late in range(2):
            pieces = [
                mid_ref[pl.ds(size * g + late, size), i].reshape(size * CH, CH) for i in range(6)
            ]
            terms.append(
                jnp.dot(
                    jnp.concatenate(pieces, axis=1),
                    wr_ref[pl.ds(6 * CH * late, 6 * CH), :],
                    preferred_element_type=jnp.float32,
                )
            )
        spread = terms[0] + terms[1]
        for q in range(size):
            for j in range(2):
                row = 2 * (g * size + q) + j
                part = spread[q * CH : (q + 1) * CH, j * CH : (j + 1) * CH]
                mid = mid_ref[size * g + q + j, 4 - 3 * j].astype(jnp.float32)
                slope = slope_ref[row].astype(jnp.float32)
                out_v[row] = (scale * (mid + slope * part)).astype(jnp.bfloat16)
            if q % 4 == 3:
                done = pl.ds(2 * (g * size + q) - 6, 8)
                pltpu.make_async_copy(out_v.at[done], out.at[0, done], out_sem).start()
        return carry

    lax.fori_loop(0, 8 * ns // size, step, 0)
    pltpu.make_async_copy(out_v, out.at[0], out_sem).wait()


def local(
    nd,
    nh,
    ns,
    features,
    row_map,
    head_weights,
    ln_gain,
    ln_bias,
    head_in,
    head_bias,
    head_out,
    patch_embed,
    act_in,
    act_mid,
    res_conv,
    out_conv,
):
    C = features.shape[-1]
    HID = head_in.shape[-1]
    rows = ns * PATCH
    group = nh * ns
    patches = ns * nh * STRIP
    order = [s % ns for s in (2, -2, 3, -3, 4, 1, -1)]
    order = [s for i, s in enumerate(order) if s and s not in order[:i]] + [0]
    per = max(1, ns // 2)
    f32, bf16 = jnp.float32, jnp.bfloat16
    vmem = pl.BlockSpec(memory_space=pltpu.VMEM)
    smem = pl.BlockSpec(memory_space=pltpu.SMEM)
    hbm = pl.BlockSpec(memory_space=pl.ANY)
    dma = pltpu.SemaphoreType.DMA
    mid, slope, wr, total = pl.pallas_call(
        functools.partial(trunk_kernel, nd, nh, ns, order, per),
        out_shape=(
            pltpu.VMEM((8 * ns + 1, 6, CH, CH), bf16),
            pltpu.VMEM((rows, CH, CH), bf16),
            pltpu.VMEM((12 * CH, 2 * CH), bf16),
            pltpu.VMEM((8, 128), f32),
        ),
        in_specs=[smem] + [pl.BlockSpec(memory_space=pltpu.HBM)] * 12,
        out_specs=(vmem,) * 4,
        scratch_shapes=[
            pltpu.SMEM(row_map.shape, jnp.int32),
            pltpu.VMEM(features.shape[1:], bf16),
            pltpu.VMEM((C, HID), bf16),
            pltpu.VMEM((P3, C), bf16),
            pltpu.VMEM((P3, PATCH * 64), bf16),
            pltpu.VMEM((C,), f32),
            pltpu.VMEM((C,), f32),
            pltpu.VMEM((1, HID), f32),
            pltpu.VMEM((1, HID), f32),
            pltpu.VMEM(res_conv.shape, bf16),
            pltpu.VMEM((3, 3, 3, CH), bf16),
            pltpu.VMEM((304, CH), f32),
            pltpu.VMEM((PATCH, 256, CH), bf16),
            pltpu.VMEM((rows, CH, CH), bf16),
            pltpu.VMEM((patches, C), bf16),
            pltpu.VMEM((patches, C), f32),
            pltpu.VMEM((rows * 16, CH), f32),
            pltpu.VMEM((ns, nh, 16, HALF), bf16),
            pltpu.VMEM((group, 16, HALF), bf16),
            pltpu.VMEM((2, rows, CH), bf16),
            pltpu.VMEM((2, CH, CH), bf16),
            pltpu.VMEM((2, rows, CH), bf16),
            pltpu.VMEM((4, 16, CH), bf16),
            pltpu.VMEM((2, CH, CH), f32),
            pltpu.VMEM((2, rows + 32, CH), f32),
            pltpu.VMEM((8, 16, HALF), bf16),
            pltpu.VMEM((8, 16, HALF), bf16),
            pltpu.VMEM((8 * ns, P3), f32),
            pltpu.VMEM((64, P3), f32),
            pltpu.VMEM((ns + 2, PADC, 128), f32),
            pltpu.VMEM((ns + 1, PADC, 128), f32),
            pltpu.VMEM((2 * PATCH, 144, 128), f32),
            pltpu.VMEM((64 * ns, 256), bf16),
            pltpu.VMEM((4 * ns, 32, 128), f32),
            pltpu.VMEM((nh, 8, 128), f32),
            pltpu.VMEM((nd * ns, 8, 128), f32),
            dma((10,)),
            dma((2,)),
            dma,
            dma,
            dma((8,)),
            dma((8,)),
            dma((8,)),
            dma((8,)),
            dma((4,)),
        ],
        compiler_params=pltpu.CompilerParams(
            collective_id=0, has_side_effects=True, vmem_limit_bytes=40 * 1024 * 1024
        ),
    )(
        head_weights,
        row_map,
        features,
        ln_gain,
        ln_bias,
        head_in,
        head_bias,
        head_out,
        patch_embed,
        act_in,
        act_mid,
        res_conv,
        out_conv.transpose(0, 1, 3, 2),
    )
    return pl.pallas_call(
        functools.partial(decode_kernel, ns, float(nd * ns * ns * nh * STRIP * P3)),
        out_shape=jax.ShapeDtypeStruct(act_in.shape, bf16),
        in_specs=[vmem] * 4,
        out_specs=hbm,
        scratch_shapes=[pltpu.VMEM((rows, CH, CH), bf16), dma],
        compiler_params=pltpu.CompilerParams(vmem_limit_bytes=16 * 1024 * 1024),
    )(mid, slope, wr, total)


def solution(mesh):
    nd, nh, ns = mesh.shape["dp"], mesh.shape["head"], mesh.shape["space"]
    in_specs = (
        P("dp", "space", None, None),
        P(),
        P("dp", "head"),
        P(),
        P(),
        P("head", None, None),
        P("head", None),
        P("head", None),
        P(),
        P("dp", "space", "head", None),
        P("dp", "space", "head", None),
        P(),
        P(),
    )
    out_specs = P("dp", "space", "head", None)
    return jax.shard_map(
        functools.partial(local, nd, nh, ns),
        mesh=mesh,
        in_specs=in_specs,
        out_specs=out_specs,
        check_vma=False,
    )
```

```python
import functools

import jax
import jax.numpy as jnp
from jax import lax
from jax.experimental import pallas as pl
from jax.experimental.pallas import tpu as pltpu
from jax.sharding import PartitionSpec as P

MESH = pl.DeviceIdType.MESH
PATCH = 16
P3 = 768
HALF = 384
CH = 128
STRIP = 8
PADC = 160
NT = (((1,), (1,)), ((), ()))
SIDES = ((0, 1), (0, -1), (1, 0), (-1, 0), (1, 1), (-1, 1), (1, -1), (-1, -1))


def gelu_slope(v):
    bell = jnp.exp(-0.5 * v * v)
    t = 1.0 / (1.0 + 0.2316418882663604 * jnp.abs(v))
    poly = t * (
        0.127414796
        + t * (-0.142248368 + t * (0.7107068705 + t * (-0.7265760135 + t * 0.5307027145)))
    )
    tail = poly * bell
    return jnp.where(v >= 0, 1.0 - tail, tail) + v * bell * 0.3989422804014327


def silu_slope(v):
    half = 0.5 * v.astype(jnp.float32)
    t = jnp.tanh(half)
    return (0.5 + 0.5 * t) * (1.0 + half * (1.0 - t))


def stack(values):
    return jnp.concatenate([values[:, :HALF], values[:, HALF:]], axis=0)


def unstack(values):
    return jnp.concatenate([values[:8], values[8:]], axis=1)


def trunk_kernel(
    nd,
    nh,
    ns,
    order,
    chunks,
    weight,
    map_hbm,
    feats,
    gain_hbm,
    shift_hbm,
    w_hbm,
    hb_hbm,
    ho_hbm,
    e_hbm,
    act_in,
    act_mid,
    res_hbm,
    tap_hbm,
    mid_out,
    slope_out,
    wr_out,
    part_out,
    total_out,
    row_map,
    f_v,
    w_v,
    e_v,
    t_v,
    g_v,
    b_v,
    hb_v,
    ho_v,
    res_v,
    tap_v,
    band_f,
    band_v,
    am_v,
    normed_v,
    unit_v,
    strip_f,
    send,
    recv,
    colmsg,
    rowland,
    colland,
    cornerland,
    sdrow,
    sdcol,
    hmsg,
    hland,
    pm,
    hp,
    x_v,
    line_f,
    row_f,
    edge_v,
    fix_f,
    sq1,
    sq2,
    load_sem,
    act_sem,
    send_sem,
    recv_sem,
    asend_sem,
    arecv_sem,
    hsend_sem,
    hrecv_sem,
    q_sem,
):
    dp, hd, sp = lax.axis_index("dp"), lax.axis_index("head"), lax.axis_index("space")
    rows = ns * PATCH
    group = nh * ns
    me = hd * ns + sp
    barrier = pltpu.get_barrier_semaphore()
    def load(src, dst, i):
        return pltpu.make_async_copy(src, dst, load_sem.at[i])

    load_map = load(map_hbm, row_map, 0)
    load_f = load(feats.at[0], f_v, 1)
    load_g = load(gain_hbm, g_v, 2)
    load_b = load(shift_hbm, b_v, 3)
    load_w = load(w_hbm.at[0], w_v, 4)
    load_hb = load(hb_hbm, hb_v, 5)
    load_ho = load(ho_hbm, ho_v, 6)
    load_e = load(e_hbm, e_v, 7)
    load_res = load(res_hbm, res_v, 8)
    load_tap = load(tap_hbm, tap_v, 9)
    load_mid = pltpu.make_async_copy(act_mid.at[0], am_v, act_sem.at[0])
    load_in = pltpu.make_async_copy(act_in.at[0], slope_out, act_sem.at[1])
    for one in (load_map, load_f, load_g, load_b, load_w, load_hb, load_ho, load_e):
        one.start()

    for i in range(1, group):
        place = (dp, lax.rem(hd + i // ns, nh), lax.rem(sp + i % ns, ns))
        pl.semaphore_signal(barrier, inc=1, device_id=place, device_id_type=MESH)
    for i in range(ns, nd * ns):
        place = (lax.rem(dp + i // ns, nd), hd, lax.rem(sp + i % ns, ns))
        pl.semaphore_signal(barrier, inc=1, device_id=place, device_id_type=MESH)

    load_map.wait()
    load_g.wait()
    load_b.wait()
    load_f.wait()
    gain = g_v[...].reshape(1, -1)
    shift = b_v[...].reshape(1, -1)
    cols = nh * STRIP

    def position(k):
        found = jnp.int32(0)
        for p in range(ns):
            found = found + jnp.where(lax.div(row_map[sp * ns + p], ns) == k, p, 0)
        return jnp.minimum(found, ns - 1)

    inverses = []
    for i, step in enumerate(order):
        values = f_v[position(lax.rem(sp + step, ns))].astype(jnp.float32)
        centred = values - jnp.mean(values, -1, keepdims=True)
        inverse = lax.rsqrt(jnp.mean(centred * centred, -1, keepdims=True) + 1e-06)
        unit = centred * inverse
        unit_v[pl.ds(i * cols, cols), :] = unit
        normed_v[pl.ds(i * cols, cols), :] = (unit * gain + shift).astype(jnp.bfloat16)
        inverses.append(inverse)

    load_hb.wait()
    load_ho.wait()
    second = ho_v[...] * weight[0, 0].astype(jnp.float32)
    first_bias = hb_v[...]
    load_w.wait()

    def send_rows(i):
        k = lax.rem(sp + order[i], ns)
        for j in range(nh):
            h = lax.rem(hd + j, nh)
            if order[i] == 0 and j == 0:
                recv[me] = send[i, h]
            else:
                pltpu.make_async_remote_copy(
                    src_ref=send.at[i, h],
                    dst_ref=recv.at[me],
                    send_sem=send_sem,
                    recv_sem=recv_sem,
                    device_id=(dp, h, k),
                    device_id_type=MESH,
                ).start()

    for chunk, (start, per) in enumerate(chunks):
        part = pl.ds(start * cols, per * cols)
        hidden = (
            jnp.dot(normed_v[part, :], w_v[...], preferred_element_type=jnp.float32) + first_bias
        )
        slopes = (second * gelu_slope(hidden)).astype(jnp.bfloat16)
        scaled = lax.dot_general(slopes, w_v[...], NT, preferred_element_type=jnp.float32) * gain
        unit = unit_v[part, :]
        inverse = jnp.concatenate(inverses[start : start + per], axis=0)
        patch = inverse * (
            scaled
            - jnp.mean(scaled, -1, keepdims=True)
            - unit * jnp.mean(scaled * unit, -1, keepdims=True)
        )
        if chunk == 0:
            load_e.wait()
            for one in (load_res, load_tap):
                one.start()
            load_mid.start()
            load_in.start()
        pixels = lax.dot_general(
            patch.astype(jnp.bfloat16), e_v[...], NT, preferred_element_type=jnp.float32
        )
        for t in range(per):
            for h in range(nh):
                at = (t * nh + h) * STRIP
                send[start + t, h] = stack(pixels[at : at + STRIP]).astype(jnp.bfloat16)
        if chunk == 0:
            pl.semaphore_wait(barrier, group - 1 + (nd - 1) * ns)
        for t in range(per):
            send_rows(start + t)

    def present(dh, ds):
        inside = jnp.bool_(True)
        if dh != 0:
            inside = jnp.logical_and(inside, hd != (0 if dh > 0 else nh - 1))
        if ds != 0:
            inside = jnp.logical_and(inside, sp != (0 if ds > 0 else ns - 1))
        return jnp.where(inside, 1.0, 0.0).astype(jnp.float32)

    load_mid.wait()

    def slope_mid(i, carry):
        am_v[pl.ds(4 * i, 4)] = silu_slope(am_v[pl.ds(4 * i, 4)]).astype(jnp.bfloat16)
        return carry

    lax.fori_loop(0, rows // 4, slope_mid, 0)
    for side in range(2):
        edge = am_v[:, pl.ds((CH - 16) * side, 16), :].astype(jnp.float32)
        strip_f[...] = edge.reshape(rows * 16, CH)
        colmsg[side] = strip_f[pl.ds(15 * side, rows, stride=16), :].astype(jnp.bfloat16)
    load_in.wait()

    def slope_in(i, carry):
        slope_out[pl.ds(4 * i, 4)] = silu_slope(slope_out[pl.ds(4 * i, 4)]).astype(jnp.bfloat16)
        return carry

    lax.fori_loop(0, rows // 4, slope_in, 0)

    line = lax.broadcasted_iota(jnp.int32, (256, 128), 0)
    goal = lax.rem(line, 16) * 64 + 6 + 3 * lax.div(line, 16)
    goal = goal - lax.broadcasted_iota(jnp.int32, (256, 128), 1)
    for o in range(3):
        for i in range(8):
            t_v[pl.ds(256 * o, 256), pl.ds(128 * i, 128)] = jnp.where(
                goal == 128 * i - o, 1.0, 0.0
            ).astype(jnp.bfloat16)

    load_tap.wait()
    load_res.wait()
    band_f[...] = jnp.zeros(band_f.shape, jnp.float32)
    for a in range(3):
        for b in range(3):
            band_f[pl.ds(48 + 64 * b + 3 * a, 3), :] = tap_v[2 - a, 2 - b].astype(jnp.float32)
    for i in range(PATCH):
        band_v[i] = band_f[pl.ds(48 - 3 * i, 256), :].astype(jnp.bfloat16)
    for i in range(4):
        for j in range(2):
            for b in range(3):
                a = i - j
                if 0 <= a <= 2:
                    block = res_v[2 - a, 2 - b].astype(jnp.float32).T.astype(jnp.bfloat16)
                else:
                    block = jnp.zeros((CH, CH), jnp.bfloat16)
                wr_out[pl.ds((i * 3 + b) * CH, CH), pl.ds(j * CH, CH)] = block

    wanted = []
    for s in range(ns):
        r = jnp.int32(0)
        for p in range(ns):
            entry = row_map[s * ns + p]
            r = r + jnp.where(lax.div(entry, ns) == sp, lax.rem(entry, ns), 0)
        wanted.append(r)
    everything = pltpu.make_async_copy(
        recv.at[pl.ds(0, group - 1)], recv.at[pl.ds(0, group - 1)], recv_sem
    )
    everything.wait()
    squares = jnp.zeros((16, HALF), jnp.float32)
    for r in range(ns):
        source = jnp.int32(0)
        for s in range(ns):
            source = source + jnp.where(wanted[s] == r, s, 0)
        source = jnp.minimum(source, ns - 1)
        summed = recv[source].astype(jnp.float32)
        for h in range(1, nh):
            summed = summed + recv[h * ns + source].astype(jnp.float32)
        squares = squares + summed * summed
        pm[pl.ds(8 * r, 8), :] = unstack(summed)

    lines = jnp.zeros((8, P3), jnp.float32)
    for d, (dh, ds) in enumerate(SIDES):
        r = ns - 1 if ds > 0 else 0
        q = STRIP - 1 if dh > 0 else 0
        if dh == 0:
            message = pm[pl.ds(8 * r, 8), :]
        elif ds == 0:
            parts = [pm[pl.ds(8 * i + q, 1), :] for i in range(ns)]
            if ns < 8:
                parts.append(lines[: 8 - ns])
            message = jnp.concatenate(parts, axis=0)
        else:
            message = jnp.broadcast_to(pm[pl.ds(8 * r + q, 1), :], (8, P3))
        hmsg[d] = stack(message).astype(jnp.bfloat16)
    halo_copies = []
    for d, (dh, ds) in enumerate(SIDES):
        halo_copies.append(
            pltpu.make_async_remote_copy(
                src_ref=hmsg.at[d],
                dst_ref=hland.at[d],
                send_sem=hsend_sem.at[d],
                recv_sem=hrecv_sem.at[d],
                device_id=(dp, lax.rem(hd + dh + nh, nh), lax.rem(sp + ds + ns, ns)),
                device_id_type=MESH,
            )
        )
    for copy in halo_copies:
        copy.start()

    squares = squares[:8] + squares[8:]
    sq1[hd] = squares[:, :128] + squares[:, 128:256] + squares[:, 256:]
    for j in range(1, nh):
        pltpu.make_async_remote_copy(
            src_ref=sq1.at[hd],
            dst_ref=sq1.at[hd],
            send_sem=q_sem.at[0],
            recv_sem=q_sem.at[1],
            device_id=(dp, lax.rem(hd + j, nh), sp),
            device_id_type=MESH,
        ).start()

    act_copies = []
    for d, (dh, ds) in enumerate(SIDES):
        if dh == 0:
            src, dst = am_v.at[rows - 1 if ds > 0 else 0], rowland.at[d]
        elif ds == 0:
            src, dst = colmsg.at[1 if dh > 0 else 0], colland.at[d - 2]
        else:
            src = am_v.at[rows - 1 if ds > 0 else 0, pl.ds(CH - 16 if dh > 0 else 0, 16)]
            dst = cornerland.at[d - 4]
        act_copies.append(
            pltpu.make_async_remote_copy(
                src_ref=src,
                dst_ref=dst,
                send_sem=asend_sem.at[d],
                recv_sem=arecv_sem.at[d],
                device_id=(dp, lax.rem(hd + dh + nh, nh), lax.rem(sp + ds + ns, ns)),
                device_id_type=MESH,
            )
        )
    for copy in act_copies:
        copy.start()

    low = lax.broadcasted_iota(jnp.int32, (8, 128), 1) < 64

    def lanes_of(spread, at, b):
        tile = spread[at : at + 8, 128 * (b // 2) : 128 * (b // 2) + 128]
        if b % 2:
            tile = pltpu.roll(tile, 64, 1)
        return jnp.where(low, tile, 0.0)

    spread = jnp.dot(pm[...].astype(jnp.bfloat16), t_v[...], preferred_element_type=jnp.float32)
    for b in range(PATCH):
        for r in range(ns):
            x_v[r + 1, pl.ds(16 + b, 8, stride=16), :] = lanes_of(spread, 8 * r, b)

    x_v[0] = jnp.zeros((PADC, 128), jnp.float32)
    lane = lax.broadcasted_iota(jnp.int32, (PADC, 128), 1)

    def set_line(block, u):
        line_f[u] = jnp.where(lane < 6, pltpu.roll(x_v[block], 80, 1), x_v[block + 1])

    def left_side(u, start, size):
        return jnp.concatenate(
            [
                line_f[u, pl.ds(start - 1, size), :]
                + pltpu.roll(line_f[u, pl.ds(start, size), :], 64, 1),
                line_f[u, pl.ds(start + 1, size), :],
            ],
            axis=1,
        ).astype(jnp.bfloat16)

    def inner(step, carry):
        block = 2 * step
        for u in range(2):
            set_line(block + u, u)
        lhs = jnp.concatenate([left_side(u, 16, CH) for u in range(2)], axis=0)
        for t in range(8):
            band = jnp.concatenate([band_v[2 * t], band_v[2 * t + 1]], axis=1)
            act = jnp.dot(lhs, band, preferred_element_type=jnp.float32)
            for u in range(2):
                for i in range(2):
                    slot = 2 * t + i
                    r = jnp.maximum((block + u) * PATCH + slot - 1, 0)
                    spot = u * PATCH + slot
                    row_f[spot, pl.ds(8, CH), :] = act[
                        CH * u : CH * u + CH, i * CH : (i + 1) * CH
                    ] * am_v[r].astype(jnp.float32)
                    for b in range(3):
                        mid_out[(block + u) * 8 + t, i * 3 + b] = row_f[
                            spot, pl.ds(7 + b, CH), :
                        ].astype(jnp.bfloat16)
        return carry

    row_f[:, pl.ds(0, 8), :] = jnp.zeros((2 * PATCH, 8, 128), jnp.float32)
    row_f[:, pl.ds(8 + CH, 8), :] = jnp.zeros((2 * PATCH, 8, 128), jnp.float32)
    lax.fori_loop(0, ns // 2, inner, 0)

    early, pairs = 2 * ns, 3 * ns

    def convolve(begin, count, where):
        terms = []
        for late in range(2):
            pieces = [
                jnp.concatenate(
                    [
                        mid_out[pl.ds(begin + late, count), i, w, :].reshape(-1, CH)
                        for w in where
                    ],
                    axis=0,
                )
                for i in range(6)
            ]
            terms.append(
                jnp.dot(
                    jnp.concatenate(pieces, axis=1),
                    wr_out[pl.ds(6 * CH * late, 6 * CH), :],
                    preferred_element_type=jnp.float32,
                )
            )
        return terms[0] + terms[1]

    def conv_early(g, carry):
        spread = convolve(early + g * ns, ns, [pl.ds(0, CH)])
        part_out[pl.ds(g * ns, ns)] = spread.reshape(ns, CH, 2 * CH)
        return carry

    lax.fori_loop(0, 1, conv_early, 0)

    seven = sq1.at[pl.ds(0, nh - 1)]
    pltpu.make_async_copy(seven, seven, q_sem.at[1]).wait()
    mine = dp * ns + sp
    sq2[mine] = jnp.sum(sq1[...], axis=0)
    for j in range(1, nd * ns):
        other = lax.rem(mine + j, nd * ns)
        pltpu.make_async_remote_copy(
            src_ref=sq2.at[mine],
            dst_ref=sq2.at[mine],
            send_sem=q_sem.at[2],
            recv_sem=q_sem.at[3],
            device_id=(lax.div(other, ns), hd, lax.rem(other, ns)),
            device_id_type=MESH,
        ).start()

    lax.fori_loop(1, pairs // ns, conv_early, 0)

    for copy in halo_copies:
        copy.wait_recv()
    for d, (dh, ds) in enumerate(SIDES):
        hp[pl.ds(8 * d, 8), :] = unstack(hland[d].astype(jnp.float32) * present(dh, ds))
    spread = jnp.dot(hp[...].astype(jnp.bfloat16), t_v[...], preferred_element_type=jnp.float32)
    for d, (dh, ds) in enumerate(SIDES):
        r = 0 if ds > 0 else ns + 1
        if dh == 0:
            for b in range(PATCH):
                x_v[r, pl.ds(16 + b, 8, stride=16), :] = lanes_of(spread, 8 * d, b)
            continue
        for b in (PATCH - 2, PATCH - 1) if dh > 0 else (0, 1):
            column = b if dh > 0 else 16 + CH + b
            tile = lanes_of(spread, 8 * d, b)
            if ds != 0:
                x_v[r, pl.ds(column, 1), :] = tile[:1]
                continue
            for i in range(ns):
                x_v[i + 1, pl.ds(column, 1), :] = tile[i : i + 1]
    for copy in act_copies:
        copy.wait_recv()
    for d, (dh, ds) in enumerate(SIDES):
        there = present(dh, ds)
        if dh == 0:
            sdrow[d] = rowland[d].astype(jnp.float32) * there
        elif ds == 0:
            sdcol[d - 2, pl.ds(16, rows), :] = colland[d - 2].astype(jnp.float32) * there
        else:
            tile = cornerland[d - 4].astype(jnp.float32) * there
            line = 15 if dh > 0 else 0
            sdcol[0 if dh > 0 else 1, pl.ds(15 if ds > 0 else 16 + rows, 1), :] = tile[
                line : line + 1
            ]

    for block in range(ns):
        set_line(block, block)
        for side in range(2):
            edge_v[pl.ds(64 * block + 32 * side, 32), :] = left_side(block, 8 + 112 * side, 32)

    def edges(t, carry):
        band = jnp.concatenate([band_v[2 * t], band_v[2 * t + 1]], axis=1)
        act = jnp.dot(edge_v[...], band, preferred_element_type=jnp.float32)
        for block in range(ns):
            for i in range(2):
                row = block * PATCH + 2 * t + i - 1
                inside = jnp.maximum(row, 0)
                for side in range(2):
                    spot = (block * 2 + i) * 2 + side
                    at = 64 * block + 32 * side
                    grad = act[at : at + 32, i * CH : (i + 1) * CH]
                    slope = am_v[inside, pl.ds((CH - 32) * side, 32), :].astype(jnp.float32)
                    beyond = sdcol[side, pl.ds(row + 16, 1), :]
                    if side == 0:
                        fix_f[spot, pl.ds(0, 8), :] = grad[:8] * beyond
                        fix_f[spot, pl.ds(8, 24), :] = grad[8:] * slope[:24]
                    else:
                        fix_f[spot, pl.ds(0, 24), :] = grad[:24] * slope[8:]
                        fix_f[spot, pl.ds(24, 8), :] = grad[24:] * beyond
                    for b in range(3):
                        mid_out[block * 8 + t, i * 3 + b, pl.ds((CH - 16) * side, 16), :] = fix_f[
                            spot, pl.ds(7 + b, 16), :
                        ].astype(jnp.bfloat16)
        return carry

    for t in range(8):
        edges(t, 0)

    set_line(ns, ns)
    band = jnp.concatenate([band_v[0], band_v[1]], axis=1)
    lhs = jnp.concatenate([left_side(0, 8, 144), left_side(ns, 8, 144)], axis=0)
    act = jnp.dot(lhs, band, preferred_element_type=jnp.float32)
    for u in range(2):
        for i in range(2):
            row = u * rows + i - 1
            grad = act[144 * u : 144 * u + 144, i * CH : (i + 1) * CH]
            if u == i:
                slope = sdrow[u]
            else:
                slope = am_v[row].astype(jnp.float32)
            spot = 2 * u + i
            row_f[spot, pl.ds(0, 8), :] = grad[:8] * sdcol[0, pl.ds(row + 16, 1), :]
            row_f[spot, pl.ds(8, CH), :] = grad[8 : 8 + CH] * slope
            row_f[spot, pl.ds(8 + CH, 8), :] = grad[8 + CH :] * sdcol[1, pl.ds(row + 16, 1), :]
            for b in range(3):
                mid_out[u * ns * 8, i * 3 + b] = row_f[spot, pl.ds(7 + b, CH), :].astype(
                    jnp.bfloat16
                )

    strips = convolve(early, pairs, [pl.ds(0, 16), pl.ds(CH - 16, 16)])
    for side in range(2):
        part_out[:, pl.ds((CH - 16) * side, 16), :] = strips[
            side * pairs * 16 : (side + 1) * pairs * 16
        ].reshape(pairs, 16, 2 * CH)

    rest = sq2.at[pl.ds(0, nd * ns - 1)]
    pltpu.make_async_copy(rest, rest, q_sem.at[3]).wait()
    total_out[...] = jnp.sum(sq2[...], axis=0)
    for copy in halo_copies + act_copies:
        copy.wait_send()
    pltpu.make_async_copy(rest, rest, q_sem.at[2]).wait()
    pltpu.make_async_copy(seven, seven, q_sem.at[0]).wait()
    pltpu.make_async_copy(
        recv.at[pl.ds(0, group - 1)], recv.at[pl.ds(0, group - 1)], send_sem
    ).wait()


def decode_kernel(ns, entries, mid_ref, slope_ref, wr_ref, part_ref, total, out, out_v, out_sem):
    scale = lax.rsqrt(jnp.sum(total[...], keepdims=True) / entries + 1e-06)
    early, pairs = 2 * ns, 3 * ns

    def finish(p, pair):
        for j in range(2):
            mid = mid_ref[p + j, 4 - 3 * j].astype(jnp.float32)
            slope = slope_ref[2 * p + j].astype(jnp.float32)
            part = pair[:, j * CH : (j + 1) * CH]
            out_v[2 * p + j] = (scale * (mid + slope * part)).astype(jnp.bfloat16)
        if p % 4 == 3:
            done = pl.ds(2 * p - 6, 8)
            pltpu.make_async_copy(out_v.at[done], out.at[0, done], out_sem).start()

    ready = list(range(early, early + pairs))
    for begin, size in ((0, 2 * ns), (early + pairs, 2 * ns), (early + pairs + 2 * ns, ns)):
        terms = []
        for late in range(2):
            pieces = [
                mid_ref[pl.ds(begin + late, size), i].reshape(size * CH, CH) for i in range(6)
            ]
            terms.append(
                jnp.dot(
                    jnp.concatenate(pieces, axis=1),
                    wr_ref[pl.ds(6 * CH * late, 6 * CH), :],
                    preferred_element_type=jnp.float32,
                )
            )
        for p in ready[: pairs // 3]:
            finish(p, part_ref[p - early])
        ready = ready[pairs // 3 :]
        spread = terms[0] + terms[1]
        for q in range(size):
            finish(begin + q, spread[q * CH : (q + 1) * CH])
    pltpu.make_async_copy(out_v, out.at[0], out_sem).wait()


def local(
    nd,
    nh,
    ns,
    features,
    row_map,
    head_weights,
    ln_gain,
    ln_bias,
    head_in,
    head_bias,
    head_out,
    patch_embed,
    act_in,
    act_mid,
    res_conv,
    out_conv,
):
    C = features.shape[-1]
    HID = head_in.shape[-1]
    rows = ns * PATCH
    group = nh * ns
    patches = ns * nh * STRIP
    order = [s % ns for s in (2, -2, 3, -3, 4, 1, -1)]
    order = [s for i, s in enumerate(order) if s and s not in order[:i]] + [0]
    chunks = [(0, ns // 2), (ns // 2, ns - ns // 2)]
    f32, bf16 = jnp.float32, jnp.bfloat16
    vmem = pl.BlockSpec(memory_space=pltpu.VMEM)
    smem = pl.BlockSpec(memory_space=pltpu.SMEM)
    hbm = pl.BlockSpec(memory_space=pl.ANY)
    dma = pltpu.SemaphoreType.DMA
    mid, slope, wr, part, total = pl.pallas_call(
        functools.partial(trunk_kernel, nd, nh, ns, order, chunks),
        out_shape=(
            pltpu.VMEM((8 * ns + 1, 6, CH, CH), bf16),
            pltpu.VMEM((rows, CH, CH), bf16),
            pltpu.VMEM((12 * CH, 2 * CH), bf16),
            pltpu.VMEM((3 * ns, CH, 2 * CH), f32),
            pltpu.VMEM((8, 128), f32),
        ),
        in_specs=[smem] + [pl.BlockSpec(memory_space=pltpu.HBM)] * 12,
        out_specs=(vmem,) * 5,
        scratch_shapes=[
            pltpu.SMEM(row_map.shape, jnp.int32),
            pltpu.VMEM(features.shape[1:], bf16),
            pltpu.VMEM((C, HID), bf16),
            pltpu.VMEM((P3, C), bf16),
            pltpu.VMEM((P3, PATCH * 64), bf16),
            pltpu.VMEM((C,), f32),
            pltpu.VMEM((C,), f32),
            pltpu.VMEM((1, HID), f32),
            pltpu.VMEM((1, HID), f32),
            pltpu.VMEM(res_conv.shape, bf16),
            pltpu.VMEM((3, 3, 3, CH), bf16),
            pltpu.VMEM((304, CH), f32),
            pltpu.VMEM((PATCH, 256, CH), bf16),
            pltpu.VMEM((rows, CH, CH), bf16),
            pltpu.VMEM((patches, C), bf16),
            pltpu.VMEM((patches, C), f32),
            pltpu.VMEM((rows * 16, CH), f32),
            pltpu.VMEM((ns, nh, 16, HALF), bf16),
            pltpu.VMEM((group, 16, HALF), bf16),
            pltpu.VMEM((2, rows, CH), bf16),
            pltpu.VMEM((2, CH, CH), bf16),
            pltpu.VMEM((2, rows, CH), bf16),
            pltpu.VMEM((4, 16, CH), bf16),
            pltpu.VMEM((2, CH, CH), f32),
            pltpu.VMEM((2, rows + 32, CH), f32),
            pltpu.VMEM((8, 16, HALF), bf16),
            pltpu.VMEM((8, 16, HALF), bf16),
            pltpu.VMEM((8 * ns, P3), f32),
            pltpu.VMEM((64, P3), f32),
            pltpu.VMEM((ns + 2, PADC, 128), f32),
            pltpu.VMEM((ns + 1, PADC, 128), f32),
            pltpu.VMEM((2 * PATCH, 144, 128), f32),
            pltpu.VMEM((64 * ns, 256), bf16),
            pltpu.VMEM((4 * ns, 32, 128), f32),
            pltpu.VMEM((nh, 8, 128), f32),
            pltpu.VMEM((nd * ns, 8, 128), f32),
            dma((10,)),
            dma((2,)),
            dma,
            dma,
            dma((8,)),
            dma((8,)),
            dma((8,)),
            dma((8,)),
            dma((4,)),
        ],
        compiler_params=pltpu.CompilerParams(
            collective_id=0, has_side_effects=True, vmem_limit_bytes=40 * 1024 * 1024
        ),
    )(
        head_weights,
        row_map,
        features,
        ln_gain,
        ln_bias,
        head_in,
        head_bias,
        head_out,
        patch_embed,
        act_in,
        act_mid,
        res_conv,
        out_conv.transpose(0, 1, 3, 2),
    )
    return pl.pallas_call(
        functools.partial(decode_kernel, ns, float(nd * ns * ns * nh * STRIP * P3)),
        out_shape=jax.ShapeDtypeStruct(act_in.shape, bf16),
        in_specs=[vmem] * 5,
        out_specs=hbm,
        scratch_shapes=[pltpu.VMEM((rows, CH, CH), bf16), dma],
        compiler_params=pltpu.CompilerParams(vmem_limit_bytes=16 * 1024 * 1024),
    )(mid, slope, wr, part, total)


def solution(mesh):
    nd, nh, ns = mesh.shape["dp"], mesh.shape["head"], mesh.shape["space"]
    in_specs = (
        P("dp", "space", None, None),
        P(),
        P("dp", "head"),
        P(),
        P(),
        P("head", None, None),
        P("head", None),
        P("head", None),
        P(),
        P("dp", "space", "head", None),
        P("dp", "space", "head", None),
        P(),
        P(),
    )
    out_specs = P("dp", "space", "head", None)
    return jax.shard_map(
        functools.partial(local, nd, nh, ns),
        mesh=mesh,
        in_specs=in_specs,
        out_specs=out_specs,
        check_vma=False,
    )
```

```python
import functools

import jax
import jax.numpy as jnp
from jax import lax
from jax.experimental import pallas as pl
from jax.experimental.pallas import tpu as pltpu
from jax.sharding import PartitionSpec as P

MESH = pl.DeviceIdType.MESH
PATCH = 16
P3 = 768
HALF = 384
CH = 128
STRIP = 8
PADC = 160
NT = (((1,), (1,)), ((), ()))
SIDES = ((0, 1), (0, -1), (1, 0), (-1, 0), (1, 1), (-1, 1), (1, -1), (-1, -1))


def gelu_slope(v):
    bell = jnp.exp(-0.5 * v * v)
    t = 1.0 / (1.0 + 0.2316418882663604 * jnp.abs(v))
    poly = t * (
        0.127414796
        + t * (-0.142248368 + t * (0.7107068705 + t * (-0.7265760135 + t * 0.5307027145)))
    )
    tail = poly * bell
    return jnp.where(v >= 0, 1.0 - tail, tail) + v * bell * 0.3989422804014327


def silu_slope(v):
    half = 0.5 * v.astype(jnp.float32)
    t = jnp.tanh(half)
    return (0.5 + 0.5 * t) * (1.0 + half * (1.0 - t))


def stack(values):
    return jnp.concatenate([values[:, :HALF], values[:, HALF:]], axis=0)


def unstack(values):
    return jnp.concatenate([values[:8], values[8:]], axis=1)


def trunk_kernel(
    nd,
    nh,
    ns,
    order,
    chunks,
    weight,
    map_hbm,
    feats,
    gain_hbm,
    shift_hbm,
    w_hbm,
    hb_hbm,
    ho_hbm,
    e_hbm,
    act_in,
    act_mid,
    res_hbm,
    tap_hbm,
    mid_out,
    slope_out,
    wr_out,
    part_out,
    total_out,
    row_map,
    f_v,
    w_v,
    e_v,
    t_v,
    g_v,
    b_v,
    hb_v,
    ho_v,
    res_v,
    tap_v,
    band_f,
    band_v,
    am_v,
    normed_v,
    unit_v,
    strip_f,
    send,
    recv,
    colmsg,
    rowland,
    colland,
    cornerland,
    sdrow,
    sdcol,
    hmsg,
    hland,
    pm,
    hp,
    x_v,
    line_f,
    row_f,
    edge_v,
    fix_f,
    sq1,
    sq2,
    load_sem,
    act_sem,
    send_sem,
    recv_sem,
    asend_sem,
    arecv_sem,
    hsend_sem,
    hrecv_sem,
    q_sem,
):
    dp, hd, sp = lax.axis_index("dp"), lax.axis_index("head"), lax.axis_index("space")
    rows = ns * PATCH
    group = nh * ns
    me = hd * ns + sp
    barrier = pltpu.get_barrier_semaphore()
    def load(src, dst, i):
        return pltpu.make_async_copy(src, dst, load_sem.at[i])

    load_map = load(map_hbm, row_map, 0)
    load_f = load(feats.at[0], f_v, 1)
    load_g = load(gain_hbm, g_v, 2)
    load_b = load(shift_hbm, b_v, 3)
    load_w = load(w_hbm.at[0], w_v, 4)
    load_hb = load(hb_hbm, hb_v, 5)
    load_ho = load(ho_hbm, ho_v, 6)
    load_e = load(e_hbm, e_v, 7)
    load_res = load(res_hbm, res_v, 8)
    load_tap = load(tap_hbm, tap_v, 9)
    load_mid = pltpu.make_async_copy(act_mid.at[0], am_v, act_sem.at[0])
    load_in = pltpu.make_async_copy(act_in.at[0], slope_out, act_sem.at[1])
    for one in (load_map, load_f, load_g, load_b, load_w, load_hb, load_ho, load_e):
        one.start()

    for i in range(1, group):
        place = (dp, lax.rem(hd + i // ns, nh), lax.rem(sp + i % ns, ns))
        pl.semaphore_signal(barrier, inc=1, device_id=place, device_id_type=MESH)
    for i in range(ns, nd * ns):
        place = (lax.rem(dp + i // ns, nd), hd, lax.rem(sp + i % ns, ns))
        pl.semaphore_signal(barrier, inc=1, device_id=place, device_id_type=MESH)

    load_map.wait()
    load_g.wait()
    load_b.wait()
    load_f.wait()
    gain = g_v[...].reshape(1, -1)
    shift = b_v[...].reshape(1, -1)
    cols = nh * STRIP

    def position(k):
        found = jnp.int32(0)
        for p in range(ns):
            found = found + jnp.where(lax.div(row_map[sp * ns + p], ns) == k, p, 0)
        return jnp.minimum(found, ns - 1)

    inverses = []
    for i, step in enumerate(order):
        values = f_v[position(lax.rem(sp + step, ns))].astype(jnp.float32)
        centred = values - jnp.mean(values, -1, keepdims=True)
        inverse = lax.rsqrt(jnp.mean(centred * centred, -1, keepdims=True) + 1e-06)
        unit = centred * inverse
        unit_v[pl.ds(i * cols, cols), :] = unit
        normed_v[pl.ds(i * cols, cols), :] = (unit * gain + shift).astype(jnp.bfloat16)
        inverses.append(inverse)

    load_hb.wait()
    load_ho.wait()
    second = ho_v[...] * weight[0, 0].astype(jnp.float32)
    first_bias = hb_v[...]
    load_w.wait()

    def send_rows(i):
        k = lax.rem(sp + order[i], ns)
        for j in range(nh):
            h = lax.rem(hd + j, nh)
            if order[i] == 0 and j == 0:
                recv[me] = send[i, h]
            else:
                pltpu.make_async_remote_copy(
                    src_ref=send.at[i, h],
                    dst_ref=recv.at[me],
                    send_sem=send_sem,
                    recv_sem=recv_sem,
                    device_id=(dp, h, k),
                    device_id_type=MESH,
                ).start()

    for chunk, (start, per) in enumerate(chunks):
        part = pl.ds(start * cols, per * cols)
        hidden = (
            jnp.dot(normed_v[part, :], w_v[...], preferred_element_type=jnp.float32) + first_bias
        )
        slopes = (second * gelu_slope(hidden)).astype(jnp.bfloat16)
        scaled = lax.dot_general(slopes, w_v[...], NT, preferred_element_type=jnp.float32) * gain
        unit = unit_v[part, :]
        inverse = jnp.concatenate(inverses[start : start + per], axis=0)
        patch = inverse * (
            scaled
            - jnp.mean(scaled, -1, keepdims=True)
            - unit * jnp.mean(scaled * unit, -1, keepdims=True)
        )
        if chunk == 0:
            load_e.wait()
            for one in (load_res, load_tap):
                one.start()
            load_mid.start()
            load_in.start()
        pixels = lax.dot_general(
            patch.astype(jnp.bfloat16), e_v[...], NT, preferred_element_type=jnp.float32
        )
        for t in range(per):
            for h in range(nh):
                at = (t * nh + h) * STRIP
                send[start + t, h] = stack(pixels[at : at + STRIP]).astype(jnp.bfloat16)
        if chunk == 0:
            pl.semaphore_wait(barrier, group - 1 + (nd - 1) * ns)
        for t in range(per):
            send_rows(start + t)

    def present(dh, ds):
        inside = jnp.bool_(True)
        if dh != 0:
            inside = jnp.logical_and(inside, hd != (0 if dh > 0 else nh - 1))
        if ds != 0:
            inside = jnp.logical_and(inside, sp != (0 if ds > 0 else ns - 1))
        return jnp.where(inside, 1.0, 0.0).astype(jnp.float32)

    load_mid.wait()

    def slope_mid(i, carry):
        am_v[pl.ds(4 * i, 4)] = silu_slope(am_v[pl.ds(4 * i, 4)]).astype(jnp.bfloat16)
        return carry

    lax.fori_loop(0, rows // 4, slope_mid, 0)
    for side in range(2):
        edge = am_v[:, pl.ds((CH - 16) * side, 16), :].astype(jnp.float32)
        strip_f[...] = edge.reshape(rows * 16, CH)
        colmsg[side] = strip_f[pl.ds(15 * side, rows, stride=16), :].astype(jnp.bfloat16)
    load_in.wait()

    def slope_in(i, carry):
        slope_out[pl.ds(4 * i, 4)] = silu_slope(slope_out[pl.ds(4 * i, 4)]).astype(jnp.bfloat16)
        return carry

    lax.fori_loop(0, rows // 4, slope_in, 0)

    line = lax.broadcasted_iota(jnp.int32, (256, 128), 0)
    goal = lax.rem(line, 16) * 64 + 6 + 3 * lax.div(line, 16)
    goal = goal - lax.broadcasted_iota(jnp.int32, (256, 128), 1)
    for o in range(3):
        for i in range(8):
            t_v[pl.ds(256 * o, 256), pl.ds(128 * i, 128)] = jnp.where(
                goal == 128 * i - o, 1.0, 0.0
            ).astype(jnp.bfloat16)

    load_tap.wait()
    load_res.wait()
    band_f[...] = jnp.zeros(band_f.shape, jnp.float32)
    for a in range(3):
        for b in range(3):
            band_f[pl.ds(48 + 64 * b + 3 * a, 3), :] = tap_v[2 - a, 2 - b].astype(jnp.float32)
    for i in range(PATCH):
        band_v[i] = band_f[pl.ds(48 - 3 * i, 256), :].astype(jnp.bfloat16)
    for i in range(4):
        for j in range(2):
            for b in range(3):
                a = i - j
                if 0 <= a <= 2:
                    block = res_v[2 - a, 2 - b].astype(jnp.float32).T.astype(jnp.bfloat16)
                else:
                    block = jnp.zeros((CH, CH), jnp.bfloat16)
                wr_out[pl.ds((i * 3 + b) * CH, CH), pl.ds(j * CH, CH)] = block

    wanted = []
    for s in range(ns):
        r = jnp.int32(0)
        for p in range(ns):
            entry = row_map[s * ns + p]
            r = r + jnp.where(lax.div(entry, ns) == sp, lax.rem(entry, ns), 0)
        wanted.append(r)
    everything = pltpu.make_async_copy(
        recv.at[pl.ds(0, group - 1)], recv.at[pl.ds(0, group - 1)], recv_sem
    )
    everything.wait()
    squares = jnp.zeros((16, HALF), jnp.float32)
    for r in range(ns):
        source = jnp.int32(0)
        for s in range(ns):
            source = source + jnp.where(wanted[s] == r, s, 0)
        source = jnp.minimum(source, ns - 1)
        summed = recv[source].astype(jnp.float32)
        for h in range(1, nh):
            summed = summed + recv[h * ns + source].astype(jnp.float32)
        squares = squares + summed * summed
        pm[pl.ds(8 * r, 8), :] = unstack(summed)

    lines = jnp.zeros((8, P3), jnp.float32)
    for d, (dh, ds) in enumerate(SIDES):
        r = ns - 1 if ds > 0 else 0
        q = STRIP - 1 if dh > 0 else 0
        if dh == 0:
            message = pm[pl.ds(8 * r, 8), :]
        elif ds == 0:
            parts = [pm[pl.ds(8 * i + q, 1), :] for i in range(ns)]
            if ns < 8:
                parts.append(lines[: 8 - ns])
            message = jnp.concatenate(parts, axis=0)
        else:
            message = jnp.broadcast_to(pm[pl.ds(8 * r + q, 1), :], (8, P3))
        hmsg[d] = stack(message).astype(jnp.bfloat16)
    halo_copies = []
    for d, (dh, ds) in enumerate(SIDES):
        halo_copies.append(
            pltpu.make_async_remote_copy(
                src_ref=hmsg.at[d],
                dst_ref=hland.at[d],
                send_sem=hsend_sem.at[d],
                recv_sem=hrecv_sem.at[d],
                device_id=(dp, lax.rem(hd + dh + nh, nh), lax.rem(sp + ds + ns, ns)),
                device_id_type=MESH,
            )
        )
    for copy in halo_copies:
        copy.start()

    squares = squares[:8] + squares[8:]
    sq1[hd] = squares[:, :128] + squares[:, 128:256] + squares[:, 256:]
    for j in range(1, nh):
        pltpu.make_async_remote_copy(
            src_ref=sq1.at[hd],
            dst_ref=sq1.at[hd],
            send_sem=q_sem.at[0],
            recv_sem=q_sem.at[1],
            device_id=(dp, lax.rem(hd + j, nh), sp),
            device_id_type=MESH,
        ).start()

    act_copies = []
    for d, (dh, ds) in enumerate(SIDES):
        if dh == 0:
            src, dst = am_v.at[rows - 1 if ds > 0 else 0], rowland.at[d]
        elif ds == 0:
            src, dst = colmsg.at[1 if dh > 0 else 0], colland.at[d - 2]
        else:
            src = am_v.at[rows - 1 if ds > 0 else 0, pl.ds(CH - 16 if dh > 0 else 0, 16)]
            dst = cornerland.at[d - 4]
        act_copies.append(
            pltpu.make_async_remote_copy(
                src_ref=src,
                dst_ref=dst,
                send_sem=asend_sem.at[d],
                recv_sem=arecv_sem.at[d],
                device_id=(dp, lax.rem(hd + dh + nh, nh), lax.rem(sp + ds + ns, ns)),
                device_id_type=MESH,
            )
        )
    for copy in act_copies:
        copy.start()

    low = lax.broadcasted_iota(jnp.int32, (8, 128), 1) < 64

    def lanes_of(spread, at, b):
        tile = spread[at : at + 8, 128 * (b // 2) : 128 * (b // 2) + 128]
        if b % 2:
            tile = pltpu.roll(tile, 64, 1)
        return jnp.where(low, tile, 0.0)

    spread = jnp.dot(pm[...].astype(jnp.bfloat16), t_v[...], preferred_element_type=jnp.float32)
    for b in range(PATCH):
        for r in range(ns):
            x_v[r + 1, pl.ds(16 + b, 8, stride=16), :] = lanes_of(spread, 8 * r, b)

    x_v[0] = jnp.zeros((PADC, 128), jnp.float32)
    lane = lax.broadcasted_iota(jnp.int32, (PADC, 128), 1)

    def set_line(block, u):
        line_f[u] = jnp.where(lane < 6, pltpu.roll(x_v[block], 80, 1), x_v[block + 1])

    def left_side(u, start, size):
        return jnp.concatenate(
            [
                line_f[u, pl.ds(start - 1, size), :]
                + pltpu.roll(line_f[u, pl.ds(start, size), :], 64, 1),
                line_f[u, pl.ds(start + 1, size), :],
            ],
            axis=1,
        ).astype(jnp.bfloat16)

    wide = min(4, ns)

    def inner(step, carry):
        block = wide * step
        for u in range(wide):
            set_line(block + u, u)
        lhs = jnp.concatenate([left_side(u, 16, CH) for u in range(wide)], axis=0)
        for t in range(8):
            band = jnp.concatenate([band_v[2 * t], band_v[2 * t + 1]], axis=1)
            act = jnp.dot(lhs, band, preferred_element_type=jnp.float32)
            for u in range(wide):
                for i in range(2):
                    slot = 2 * t + i
                    r = jnp.maximum((block + u) * PATCH + slot - 1, 0)
                    spot = u * PATCH + slot
                    row_f[spot, pl.ds(8, CH), :] = act[
                        CH * u : CH * u + CH, i * CH : (i + 1) * CH
                    ] * am_v[r].astype(jnp.float32)
                    for b in range(3):
                        mid_out[(block + u) * 8 + t, i * 3 + b] = row_f[
                            spot, pl.ds(7 + b, CH), :
                        ].astype(jnp.bfloat16)
        return carry

    row_f[:, pl.ds(0, 8), :] = jnp.zeros((wide * PATCH, 8, 128), jnp.float32)
    row_f[:, pl.ds(8 + CH, 8), :] = jnp.zeros((wide * PATCH, 8, 128), jnp.float32)
    lax.fori_loop(0, ns // wide, inner, 0)

    early, pairs = 2 * ns, 3 * ns

    def convolve(begin, count, where):
        terms = []
        for late in range(2):
            pieces = [
                jnp.concatenate(
                    [
                        mid_out[pl.ds(begin + late, count), i, w, :].reshape(-1, CH)
                        for w in where
                    ],
                    axis=0,
                )
                for i in range(6)
            ]
            terms.append(
                jnp.dot(
                    jnp.concatenate(pieces, axis=1),
                    wr_out[pl.ds(6 * CH * late, 6 * CH), :],
                    preferred_element_type=jnp.float32,
                )
            )
        return terms[0] + terms[1]

    def conv_early(g, carry):
        spread = convolve(early + g * ns, ns, [pl.ds(0, CH)])
        part_out[pl.ds(g * ns, ns)] = spread.reshape(ns, CH, 2 * CH)
        return carry

    lax.fori_loop(0, 1, conv_early, 0)

    seven = sq1.at[pl.ds(0, nh - 1)]
    pltpu.make_async_copy(seven, seven, q_sem.at[1]).wait()
    mine = dp * ns + sp
    sq2[mine] = jnp.sum(sq1[...], axis=0)
    for j in range(1, nd * ns):
        other = lax.rem(mine + j, nd * ns)
        pltpu.make_async_remote_copy(
            src_ref=sq2.at[mine],
            dst_ref=sq2.at[mine],
            send_sem=q_sem.at[2],
            recv_sem=q_sem.at[3],
            device_id=(lax.div(other, ns), hd, lax.rem(other, ns)),
            device_id_type=MESH,
        ).start()

    lax.fori_loop(1, pairs // ns, conv_early, 0)

    for copy in halo_copies:
        copy.wait_recv()
    for d, (dh, ds) in enumerate(SIDES):
        hp[pl.ds(8 * d, 8), :] = unstack(hland[d].astype(jnp.float32) * present(dh, ds))
    spread = jnp.dot(hp[...].astype(jnp.bfloat16), t_v[...], preferred_element_type=jnp.float32)
    for d, (dh, ds) in enumerate(SIDES):
        r = 0 if ds > 0 else ns + 1
        if dh == 0:
            for b in range(PATCH):
                x_v[r, pl.ds(16 + b, 8, stride=16), :] = lanes_of(spread, 8 * d, b)
            continue
        for b in (PATCH - 2, PATCH - 1) if dh > 0 else (0, 1):
            column = b if dh > 0 else 16 + CH + b
            tile = lanes_of(spread, 8 * d, b)
            if ds != 0:
                x_v[r, pl.ds(column, 1), :] = tile[:1]
                continue
            for i in range(ns):
                x_v[i + 1, pl.ds(column, 1), :] = tile[i : i + 1]
    for copy in act_copies:
        copy.wait_recv()
    for d, (dh, ds) in enumerate(SIDES):
        there = present(dh, ds)
        if dh == 0:
            sdrow[d] = rowland[d].astype(jnp.float32) * there
        elif ds == 0:
            sdcol[d - 2, pl.ds(16, rows), :] = colland[d - 2].astype(jnp.float32) * there
        else:
            tile = cornerland[d - 4].astype(jnp.float32) * there
            line = 15 if dh > 0 else 0
            sdcol[0 if dh > 0 else 1, pl.ds(15 if ds > 0 else 16 + rows, 1), :] = tile[
                line : line + 1
            ]

    for block in range(ns):
        set_line(block, block)
        for side in range(2):
            edge_v[pl.ds(64 * block + 32 * side, 32), :] = left_side(block, 8 + 112 * side, 32)

    def edges(t, carry):
        band = jnp.concatenate([band_v[2 * t], band_v[2 * t + 1]], axis=1)
        act = jnp.dot(edge_v[...], band, preferred_element_type=jnp.float32)
        for block in range(ns):
            for i in range(2):
                row = block * PATCH + 2 * t + i - 1
                inside = jnp.maximum(row, 0)
                for side in range(2):
                    spot = (block * 2 + i) * 2 + side
                    at = 64 * block + 32 * side
                    grad = act[at : at + 32, i * CH : (i + 1) * CH]
                    slope = am_v[inside, pl.ds((CH - 32) * side, 32), :].astype(jnp.float32)
                    beyond = sdcol[side, pl.ds(row + 16, 1), :]
                    if side == 0:
                        fix_f[spot, pl.ds(0, 8), :] = grad[:8] * beyond
                        fix_f[spot, pl.ds(8, 24), :] = grad[8:] * slope[:24]
                    else:
                        fix_f[spot, pl.ds(0, 24), :] = grad[:24] * slope[8:]
                        fix_f[spot, pl.ds(24, 8), :] = grad[24:] * beyond
                    for b in range(3):
                        mid_out[block * 8 + t, i * 3 + b, pl.ds((CH - 16) * side, 16), :] = fix_f[
                            spot, pl.ds(7 + b, 16), :
                        ].astype(jnp.bfloat16)
        return carry

    for t in range(8):
        edges(t, 0)

    set_line(ns, ns)
    band = jnp.concatenate([band_v[0], band_v[1]], axis=1)
    lhs = jnp.concatenate([left_side(0, 8, 144), left_side(ns, 8, 144)], axis=0)
    act = jnp.dot(lhs, band, preferred_element_type=jnp.float32)
    for u in range(2):
        for i in range(2):
            row = u * rows + i - 1
            grad = act[144 * u : 144 * u + 144, i * CH : (i + 1) * CH]
            if u == i:
                slope = sdrow[u]
            else:
                slope = am_v[row].astype(jnp.float32)
            spot = 2 * u + i
            row_f[spot, pl.ds(0, 8), :] = grad[:8] * sdcol[0, pl.ds(row + 16, 1), :]
            row_f[spot, pl.ds(8, CH), :] = grad[8 : 8 + CH] * slope
            row_f[spot, pl.ds(8 + CH, 8), :] = grad[8 + CH :] * sdcol[1, pl.ds(row + 16, 1), :]
            for b in range(3):
                mid_out[u * ns * 8, i * 3 + b] = row_f[spot, pl.ds(7 + b, CH), :].astype(
                    jnp.bfloat16
                )

    strips = convolve(early, pairs, [pl.ds(0, 16), pl.ds(CH - 16, 16)])
    for side in range(2):
        part_out[:, pl.ds((CH - 16) * side, 16), :] = strips[
            side * pairs * 16 : (side + 1) * pairs * 16
        ].reshape(pairs, 16, 2 * CH)

    rest = sq2.at[pl.ds(0, nd * ns - 1)]
    pltpu.make_async_copy(rest, rest, q_sem.at[3]).wait()
    total_out[...] = jnp.sum(sq2[...], axis=0)
    for copy in halo_copies + act_copies:
        copy.wait_send()
    pltpu.make_async_copy(rest, rest, q_sem.at[2]).wait()
    pltpu.make_async_copy(seven, seven, q_sem.at[0]).wait()
    pltpu.make_async_copy(
        recv.at[pl.ds(0, group - 1)], recv.at[pl.ds(0, group - 1)], send_sem
    ).wait()


def decode_kernel(ns, entries, mid_ref, slope_ref, wr_ref, part_ref, total, out, out_v, out_sem):
    scale = lax.rsqrt(jnp.sum(total[...], keepdims=True) / entries + 1e-06)
    early, pairs = 2 * ns, 3 * ns

    def finish(p, pair):
        for j in range(2):
            mid = mid_ref[p + j, 4 - 3 * j].astype(jnp.float32)
            slope = slope_ref[2 * p + j].astype(jnp.float32)
            part = pair[:, j * CH : (j + 1) * CH]
            out_v[2 * p + j] = (scale * (mid + slope * part)).astype(jnp.bfloat16)
        if p % 4 == 3:
            done = pl.ds(2 * p - 6, 8)
            pltpu.make_async_copy(out_v.at[done], out.at[0, done], out_sem).start()

    ready = list(range(early, early + pairs))
    for begin, size in ((0, 2 * ns), (early + pairs, 2 * ns), (early + pairs + 2 * ns, ns)):
        terms = []
        for late in range(2):
            pieces = [
                mid_ref[pl.ds(begin + late, size), i].reshape(size * CH, CH) for i in range(6)
            ]
            terms.append(
                jnp.dot(
                    jnp.concatenate(pieces, axis=1),
                    wr_ref[pl.ds(6 * CH * late, 6 * CH), :],
                    preferred_element_type=jnp.float32,
                )
            )
        for p in ready[: pairs // 3]:
            finish(p, part_ref[p - early])
        ready = ready[pairs // 3 :]
        spread = terms[0] + terms[1]
        for q in range(size):
            finish(begin + q, spread[q * CH : (q + 1) * CH])
    pltpu.make_async_copy(out_v, out.at[0], out_sem).wait()


def local(
    nd,
    nh,
    ns,
    features,
    row_map,
    head_weights,
    ln_gain,
    ln_bias,
    head_in,
    head_bias,
    head_out,
    patch_embed,
    act_in,
    act_mid,
    res_conv,
    out_conv,
):
    C = features.shape[-1]
    HID = head_in.shape[-1]
    rows = ns * PATCH
    group = nh * ns
    patches = ns * nh * STRIP
    order = [s % ns for s in (2, -2, 3, -3, 4, 1, -1)]
    order = [s for i, s in enumerate(order) if s and s not in order[:i]] + [0]
    chunks = [(0, ns // 2), (ns // 2, ns - ns // 2)]
    f32, bf16 = jnp.float32, jnp.bfloat16
    vmem = pl.BlockSpec(memory_space=pltpu.VMEM)
    smem = pl.BlockSpec(memory_space=pltpu.SMEM)
    hbm = pl.BlockSpec(memory_space=pl.ANY)
    dma = pltpu.SemaphoreType.DMA
    mid, slope, wr, part, total = pl.pallas_call(
        functools.partial(trunk_kernel, nd, nh, ns, order, chunks),
        out_shape=(
            pltpu.VMEM((8 * ns + 1, 6, CH, CH), bf16),
            pltpu.VMEM((rows, CH, CH), bf16),
            pltpu.VMEM((12 * CH, 2 * CH), bf16),
            pltpu.VMEM((3 * ns, CH, 2 * CH), f32),
            pltpu.VMEM((8, 128), f32),
        ),
        in_specs=[smem] + [pl.BlockSpec(memory_space=pltpu.HBM)] * 12,
        out_specs=(vmem,) * 5,
        scratch_shapes=[
            pltpu.SMEM(row_map.shape, jnp.int32),
            pltpu.VMEM(features.shape[1:], bf16),
            pltpu.VMEM((C, HID), bf16),
            pltpu.VMEM((P3, C), bf16),
            pltpu.VMEM((P3, PATCH * 64), bf16),
            pltpu.VMEM((C,), f32),
            pltpu.VMEM((C,), f32),
            pltpu.VMEM((1, HID), f32),
            pltpu.VMEM((1, HID), f32),
            pltpu.VMEM(res_conv.shape, bf16),
            pltpu.VMEM((3, 3, 3, CH), bf16),
            pltpu.VMEM((304, CH), f32),
            pltpu.VMEM((PATCH, 256, CH), bf16),
            pltpu.VMEM((rows, CH, CH), bf16),
            pltpu.VMEM((patches, C), bf16),
            pltpu.VMEM((patches, C), f32),
            pltpu.VMEM((rows * 16, CH), f32),
            pltpu.VMEM((ns, nh, 16, HALF), bf16),
            pltpu.VMEM((group, 16, HALF), bf16),
            pltpu.VMEM((2, rows, CH), bf16),
            pltpu.VMEM((2, CH, CH), bf16),
            pltpu.VMEM((2, rows, CH), bf16),
            pltpu.VMEM((4, 16, CH), bf16),
            pltpu.VMEM((2, CH, CH), f32),
            pltpu.VMEM((2, rows + 32, CH), f32),
            pltpu.VMEM((8, 16, HALF), bf16),
            pltpu.VMEM((8, 16, HALF), bf16),
            pltpu.VMEM((8 * ns, P3), f32),
            pltpu.VMEM((64, P3), f32),
            pltpu.VMEM((ns + 2, PADC, 128), f32),
            pltpu.VMEM((ns + 1, PADC, 128), f32),
            pltpu.VMEM((min(4, ns) * PATCH, 144, 128), f32),
            pltpu.VMEM((64 * ns, 256), bf16),
            pltpu.VMEM((4 * ns, 32, 128), f32),
            pltpu.VMEM((nh, 8, 128), f32),
            pltpu.VMEM((nd * ns, 8, 128), f32),
            dma((10,)),
            dma((2,)),
            dma,
            dma,
            dma((8,)),
            dma((8,)),
            dma((8,)),
            dma((8,)),
            dma((4,)),
        ],
        compiler_params=pltpu.CompilerParams(
            collective_id=0, has_side_effects=True, vmem_limit_bytes=40 * 1024 * 1024
        ),
    )(
        head_weights,
        row_map,
        features,
        ln_gain,
        ln_bias,
        head_in,
        head_bias,
        head_out,
        patch_embed,
        act_in,
        act_mid,
        res_conv,
        out_conv.transpose(0, 1, 3, 2),
    )
    return pl.pallas_call(
        functools.partial(decode_kernel, ns, float(nd * ns * ns * nh * STRIP * P3)),
        out_shape=jax.ShapeDtypeStruct(act_in.shape, bf16),
        in_specs=[vmem] * 5,
        out_specs=hbm,
        scratch_shapes=[pltpu.VMEM((rows, CH, CH), bf16), dma],
        compiler_params=pltpu.CompilerParams(vmem_limit_bytes=16 * 1024 * 1024),
    )(mid, slope, wr, part, total)


def solution(mesh):
    nd, nh, ns = mesh.shape["dp"], mesh.shape["head"], mesh.shape["space"]
    in_specs = (
        P("dp", "space", None, None),
        P(),
        P("dp", "head"),
        P(),
        P(),
        P("head", None, None),
        P("head", None),
        P("head", None),
        P(),
        P("dp", "space", "head", None),
        P("dp", "space", "head", None),
        P(),
        P(),
    )
    out_specs = P("dp", "space", "head", None)
    return jax.shard_map(
        functools.partial(local, nd, nh, ns),
        mesh=mesh,
        in_specs=in_specs,
        out_specs=out_specs,
        check_vma=False,
    )
```
